256 devices in a mesh: cluster: 256 (over x, y, z, core).
Axes of the slice: x: 4, y: 4, z: 8, core: 2. Of those that a mesh axis runs over, the one named last changes fastest.
Arguments:
- x_block: float32 [8, 131072], P(None, 'cluster'), may hold values from -6 to 6
- near_tiles: float32 [2048, 27, 64, 64], P('cluster'), may hold values from -0.15625 to 0.15625
- near_list: int32 [2048, 27], P('cluster'), may hold values from 0 to 2047, as said below
- near_count: int32 [2048], P('cluster'), may hold values from 1 to 27, as said below
- leaf_in: float32 [2048, 64, 32], P('cluster'), may hold values from -0.75 to 0.75
- leaf_up: float32 [2048, 32, 32], P('cluster'), may hold values from -0.375 to 0.375
- mid_up: float32 [256, 32, 32], P('cluster'), may hold values from -0.375 to 0.375
- leaf_tiles: float32 [2048, 48, 32, 32], P('cluster'), may hold values from -0.21875 to 0.21875
- leaf_list: int32 [2048, 48], P('cluster'), may hold values from 0 to 2047, as said below
- leaf_count: int32 [2048], P('cluster'), may hold values from 1 to 48, as said below
- mid_tiles: float32 [256, 48, 32, 32], P('cluster'), may hold values from -0.21875 to 0.21875
- mid_list: int32 [256, 48], P('cluster'), may hold values from 0 to 255, as said below
- mid_count: int32 [256], P('cluster'), may hold values from 1 to 48, as said below
- top_tiles: float32 [32, 16, 32, 32], replicated, may hold values from -0.25 to 0.25
- top_list: int32 [32, 16], replicated, may hold values from 0 to 31
- mid_down: float32 [256, 32, 32], P('cluster'), may hold values from -1 to 1
- leaf_down: float32 [2048, 32, 32], P('cluster'), may hold values from -1 to 1
- leaf_out: float32 [2048, 64, 32], P('cluster'), may hold values from -0.75 to 0.75
Outputs:
- product: float32 [8, 131072], P(None, 'cluster')
The draws below stay inside these ranges and needn't reach their ends.
Inputs may be any that keep to these rules, and one draw needn't show every extreme that they name: `near_list`: slot 0 is the leaf itself; every source leaf lies among the leaves of the target's own device block of 8 leaves and the blocks just before and after it. `near_count`: at least 1; the largest count is reached on some leaf. `leaf_list`: sources may be any leaf. `leaf_count`: loads differ from device to device; the largest count is reached on some leaf. `mid_list`: sources may be any middle cluster. `mid_count`: the largest count is reached on some middle cluster.
All inputs are finite; a program needn't handle non-finite values.
Results may differ from the reference program's by a relative error of at most 0.000061.
Values sent between devices are 32-bit elements; how exact they have to be, the bound alone decides.
A program may use at most 128 MiB of HBM per device.

```python
import jax
import jax.numpy as jnp
from jax import lax

P_SIZE = 64
R = 32
NRHS = 8
NEAR = 27
IL0 = 48
IL1 = 48
IL2 = 16
LEAF_DEV = 8
MID_DEV = 1
LEAVES = 2048
MIDS = 256
TOPS = 32
PANELS = 131072


def count_law(key, blocks, per, most):
    keys = jax.random.split(key, 4)
    caps = jax.random.randint(keys[0], (blocks,), max(most // 4, 1), most + 1)
    busiest = jax.random.randint(keys[1], (), 0, blocks)
    caps = jnp.where(jnp.arange(blocks) == busiest, most, caps)
    floor_val = jnp.maximum(caps // 2, 1)
    spread = jax.random.randint(keys[2], (blocks, per), 0, 1 << 20)
    counts = floor_val[:, None] + spread % (caps - floor_val + 1)[:, None]
    chosen = jax.random.randint(keys[3], (blocks,), 0, per)
    counts = jnp.where(jnp.arange(per)[None, :] == chosen[:, None], caps[:, None], counts)
    return counts.reshape(-1).astype(jnp.int32)


def draw_near_list(key, part):
    key = jax.random.fold_in(key, 11)
    leaves = jnp.arange(LEAVES, dtype=jnp.int32)
    base = leaves // LEAF_DEV * LEAF_DEV
    offset = jax.random.randint(key, (LEAVES, NEAR), -LEAF_DEV, 2 * LEAF_DEV)
    source = jnp.clip(base[:, None] + offset, 0, LEAVES - 1)
    source = source.at[:, 0].set(leaves)
    return source.astype(jnp.int32)


def draw_near_count(key, part):
    key = jax.random.fold_in(key, 12)
    return count_law(key, LEAVES // LEAF_DEV, LEAF_DEV, NEAR)


def draw_leaf_list(key, part):
    key = jax.random.fold_in(key, 13)
    return jax.random.randint(key, (LEAVES, IL0), 0, LEAVES).astype(jnp.int32)


def draw_leaf_count(key, part):
    key = jax.random.fold_in(key, 14)
    return count_law(key, LEAVES // LEAF_DEV, LEAF_DEV, IL0)


def draw_mid_list(key, part):
    key = jax.random.fold_in(key, 15)
    return jax.random.randint(key, (MIDS, IL1), 0, MIDS).astype(jnp.int32)


def draw_mid_count(key, part):
    key = jax.random.fold_in(key, 16)
    return count_law(key, MIDS // MID_DEV, MID_DEV, IL1)


def plant(result, stream_key, low, top_value):
    extent = result.shape
    place = [jax.random.randint(jax.random.fold_in(stream_key, axis), (), 0, extent[axis]) for axis in range(len(extent))]
    result = result.at[tuple(place)].set(low)
    longest = extent.index(max(extent))
    place[longest] = (place[longest] + 1) % extent[longest]
    return result.at[tuple(place)].set(top_value)


def steps_of(own_key, dims, cuts, smallest, high):
    def one(dim, blocks):
        draws = jax.random.uniform(jax.random.fold_in(jax.random.fold_in(own_key, 6), dim), (blocks,), jnp.float32, smallest / len(cuts), high / len(cuts))
        return jnp.repeat(jnp.exp(draws), dims[dim] // blocks).reshape((-1,) + (1,) * (len(dims) - dim - 1))

    level = one(*cuts[0])
    for cut in cuts[1:]:
        level = level * one(*cut)
    return level


def gaussian(stream_key, dims, scale, bound, shards=(), kind=jnp.bfloat16):
    gain = steps_of(stream_key, dims, shards, -0.22, 0.18) if shards else 1.0
    entries = jax.random.normal(stream_key, dims, jnp.float32) * scale * gain
    return jnp.minimum(jnp.maximum(entries, -bound), bound).astype(kind)


def setup_inputs(seed: int = 0) -> dict:
    seeds = jax.random.split(jax.random.key(seed), 19)
    x_block = gaussian(seeds[0], (NRHS, PANELS), 1.0, 6.0, ((1, 256),), jnp.float32)
    near_tiles = gaussian(seeds[1], (LEAVES, NEAR, P_SIZE, P_SIZE), (NEAR * P_SIZE) ** -0.5, 0.15625, ((0, 256),), jnp.float32)
    near_list = draw_near_list(jax.random.fold_in(seeds[18], 71), 0)
    near_count = draw_near_count(jax.random.fold_in(seeds[18], 71), 0)
    leaf_in = gaussian(seeds[4], (LEAVES, P_SIZE, R), P_SIZE ** -0.5, 0.75, ((0, 256),), jnp.float32)
    leaf_up = gaussian(seeds[5], (LEAVES, R, R), (8 * R) ** -0.5, 0.375, ((0, 256),), jnp.float32)
    mid_up = gaussian(seeds[6], (MIDS, R, R), (8 * R) ** -0.5, 0.375, ((0, 256),), jnp.float32)
    leaf_tiles = gaussian(seeds[7], (LEAVES, IL0, R, R), (IL0 * R // 2) ** -0.5, 0.21875, ((0, 256),), jnp.float32)
    leaf_list = draw_leaf_list(jax.random.fold_in(seeds[18], 71), 0)
    leaf_count = draw_leaf_count(jax.random.fold_in(seeds[18], 71), 0)
    mid_tiles = gaussian(seeds[10], (MIDS, IL1, R, R), (IL1 * R // 2) ** -0.5, 0.21875, ((0, 256),), jnp.float32)
    mid_list = draw_mid_list(jax.random.fold_in(seeds[18], 71), 0)
    mid_count = draw_mid_count(jax.random.fold_in(seeds[18], 71), 0)
    top_tiles = gaussian(seeds[13], (TOPS, IL2, R, R), (IL2 * R) ** -0.5, 0.25, (), jnp.float32)
    top_list = plant(jax.random.randint(seeds[14], (TOPS, IL2), 0, TOPS), jax.random.fold_in(seeds[14], 1), 0, TOPS - 1).astype(jnp.int32)
    mid_down = gaussian(seeds[15], (MIDS, R, R), R ** -0.5, 1.0, ((0, 256),), jnp.float32)
    leaf_down = gaussian(seeds[16], (LEAVES, R, R), R ** -0.5, 1.0, ((0, 256),), jnp.float32)
    leaf_out = gaussian(seeds[17], (LEAVES, P_SIZE, R), (2 * R) ** -0.5, 0.75, ((0, 256),), jnp.float32)
    return {"x_block": x_block, "near_tiles": near_tiles, "near_list": near_list, "near_count": near_count, "leaf_in": leaf_in, "leaf_up": leaf_up, "mid_up": mid_up, "leaf_tiles": leaf_tiles, "leaf_list": leaf_list, "leaf_count": leaf_count, "mid_tiles": mid_tiles, "mid_list": mid_list, "mid_count": mid_count, "top_tiles": top_tiles, "top_list": top_list, "mid_down": mid_down, "leaf_down": leaf_down, "leaf_out": leaf_out}


HIGH = lax.Precision.HIGHEST


def reference(x_block, near_tiles, near_list, near_count, leaf_in, leaf_up, mid_up, leaf_tiles, leaf_list, leaf_count, mid_tiles, mid_list, mid_count, top_tiles, top_list, mid_down, leaf_down, leaf_out):
    xl = x_block.reshape(NRHS, LEAVES, P_SIZE)
    near_live = (jnp.arange(NEAR)[None, :] < near_count[:, None]).astype(jnp.float32)
    picked = xl[:, near_list]
    near = jnp.einsum("lnpq,rlnp,ln->rlq", near_tiles, picked, near_live, precision=HIGH)
    leaf_coef = jnp.einsum("lpa,rlp->lar", leaf_in, xl, precision=HIGH)
    mid_coef = jnp.einsum("lab,lar->lbr", leaf_up, leaf_coef, precision=HIGH).reshape(MIDS, 8, R, NRHS).sum(1)
    top_coef = jnp.einsum("mab,mar->mbr", mid_up, mid_coef, precision=HIGH).reshape(TOPS, 8, R, NRHS).sum(1)
    top_field = jnp.einsum("tjab,tjar->tbr", top_tiles, top_coef[top_list], precision=HIGH)
    mid_live = (jnp.arange(IL1)[None, :] < mid_count[:, None]).astype(jnp.float32)
    mid_field = jnp.einsum("mjca,mjcr,mj->mar", mid_tiles, mid_coef[mid_list], mid_live, precision=HIGH)
    mid_field = mid_field + jnp.einsum("mab,mbr->mar", mid_down, jnp.repeat(top_field, 8, axis=0), precision=HIGH)
    leaf_live = (jnp.arange(IL0)[None, :] < leaf_count[:, None]).astype(jnp.float32)
    leaf_field = jnp.einsum("ljca,ljcr,lj->lar", leaf_tiles, leaf_coef[leaf_list], leaf_live, precision=HIGH)
    leaf_field = leaf_field + jnp.einsum("lab,lbr->lar", leaf_down, jnp.repeat(mid_field, 8, axis=0), precision=HIGH)
    far = jnp.einsum("lpa,lar->rlp", leaf_out, leaf_field, precision=HIGH)
    return (near + far).reshape(NRHS, PANELS)
```

```python
import functools

import jax
import jax.numpy as jnp
from jax import lax
from jax.experimental import pallas as pl
from jax.experimental.pallas import tpu as pltpu
from jax.sharding import PartitionSpec as P

F32 = jnp.float32
BF16 = jnp.bfloat16
MESH = pl.DeviceIdType.MESH

X, Y, Z = 4, 4, 8
ROWS = 80
HALF = ROWS // 2

U1P, U1M, U2P, U2M = 0, 1, 2, 3
V1P, V1M, V2P, V2M = 4, 8, 12, 16
SIB = 20
COPIES = 36


def mod(a, n):
    return lax.rem(a + n, n)


def stacked(a):
    hi = a.astype(BF16).astype(F32)
    return jnp.concatenate([hi, a - hi], axis=0).astype(BF16)


def split(b):
    hi = b.astype(BF16)
    return hi, (b - hi.astype(F32)).astype(BF16)


def dot(a, b):
    return jnp.dot(a, b, preferred_element_type=F32)


def product2(a, hi, lo):
    both = stacked(a)
    out = dot(both, hi) + dot(both, lo)
    half = out.shape[0] // 2
    return out[:half] + out[half:]


def product(a, b):
    return product2(a, *split(b))


def iota(shape, dim):
    return lax.broadcasted_iota(jnp.int32, shape, dim)


def kernel(
    near_list,
    near_count,
    leaf_count,
    mid_count,
    leaf_list,
    mid_list,
    top_list,
    x_hbm,
    near_hbm,
    leaf_hbm,
    mid_hbm,
    top_hbm,
    lin_hbm,
    lup_hbm,
    mup_hbm,
    mdn_hbm,
    ldn_hbm,
    lout_hbm,
    out_ref,
    xbuf,
    near_v,
    leaf_v,
    mid_v,
    top_v,
    lin_v,
    lup_v,
    mup_v,
    mdn_v,
    ldn_v,
    lout_v,
    coef,
    stage,
    xe,
    near_acc,
    onehot,
    onehot2,
    picked,
    whi,
    wlo,
    w2hi,
    w2lo,
    ohi,
    olo,
    load_sem,
    near_sem,
    halo_send,
    halo_recv,
    z_send,
    z_recv,
    col_send,
    col_recv,
):
    me = lax.axis_index("cluster")
    c = lax.rem(me, 2)
    z = lax.rem(lax.div(me, 2), Z)
    y = lax.rem(lax.div(me, 2 * Z), Y)
    x = lax.div(me, 2 * Z * Y)
    v = x + c * (y - x)
    u = y + c * (x - y)

    def device(vv, uu, zz):
        xx = vv + c * (uu - vv)
        yy = uu + c * (vv - uu)
        return ((xx * Y + yy) * Z + zz) * 2 + c

    sibling = me + 1 - 2 * c
    right = mod(me + 1, 256)
    left = mod(me - 1, 256)

    def load(i, source, target):
        copy = pltpu.make_async_copy(source, target, load_sem.at[i])
        copy.start()
        return copy

    load_x = load(0, x_hbm, xbuf.at[1])
    load_lin = load(1, lin_hbm, lin_v)
    load_lup = load(2, lup_hbm, lup_v)
    load_mup = load(3, mup_hbm, mup_v)
    load_near = []
    for i in range(4):
        copy = pltpu.make_async_copy(
            near_hbm.at[pl.ds(2 * i, 2)], near_v.at[pl.ds(2 * i, 2)], near_sem.at[i]
        )
        copy.start()
        load_near.append(copy)
    load_leaf = load(4, leaf_hbm, leaf_v)
    load_mid = load(5, mid_hbm, mid_v)
    load_top = load(6, top_hbm.at[lax.div(me, 8)], top_v)
    load_mdn = load(7, mdn_hbm, mdn_v)
    load_ldn = load(8, ldn_hbm, ldn_v)
    load_lout = load(9, lout_hbm, lout_v)

    barrier = pltpu.get_barrier_semaphore()
    partners = [device(v, u, mod(z + k, Z)) for k in range(1, Z)]
    up, um = mod(u + 1, 4), mod(u - 1, 4)
    vp, vm = mod(v + 1, 4), mod(v - 1, 4)
    dev_up, dev_um = device(v, up, z), device(v, um, z)
    dev_vp, dev_vm = device(vp, u, z), device(vm, u, z)
    partners += [dev_up, dev_um, dev_vp, dev_vm, sibling, right, left]
    for partner in partners:
        pl.semaphore_signal(barrier, inc=1, device_id=(partner,), device_id_type=MESH)

    load_x.wait()
    load_lin.wait()
    load_lup.wait()
    load_mup.wait()
    zeros64 = jnp.zeros((32, 64), F32)
    r_parts = []
    for i in range(4):
        block = jnp.concatenate(
            [
                jnp.concatenate([lin_v[2 * i], zeros64], axis=1),
                jnp.concatenate([zeros64, lin_v[2 * i + 1]], axis=1),
            ],
            axis=0,
        )
        hi, lo = split(block)
        both = stacked(xbuf[1, :, i * 128 : (i + 1) * 128])
        nt = functools.partial(
            lax.dot_general,
            dimension_numbers=(((1,), (1,)), ((), ())),
            preferred_element_type=F32,
        )
        part = nt(both, hi) + nt(both, lo)
        r_parts.append(part[:8] + part[8:])
    r = jnp.concatenate(r_parts, axis=1)
    lup = lup_v[...].reshape(256, 32)
    both_up = jnp.concatenate([lup, product(lup, mup_v[0])], axis=1)
    p = product(r, both_up)
    rp = jnp.concatenate([r, p, jnp.zeros((8, 64), F32)], axis=1)
    hi = rp.astype(BF16).astype(F32)
    rest = rp - hi
    mid = rest.astype(BF16).astype(F32)
    rp4 = jnp.concatenate([hi, mid, rest - mid, jnp.zeros_like(rp)], axis=0)
    spread = (iota((32, 256), 0) % 8 == iota((32, 256), 1) % 8).astype(BF16)
    rows = dot(jnp.transpose(rp4).astype(BF16), spread)
    rows = rows[:320].reshape(10, 32, 256)
    same = iota((32, 256), 0) == iota((32, 256), 1) // 8
    rows = jnp.sum(jnp.where(same[None], rows, 0.0), axis=1)
    my_rows = pl.ds(pl.multiple_of(z * 8, 8), 8)
    coef[c, v, u, my_rows, :] = rows[:8]
    stage[z] = rows[8:10]

    pl.semaphore_wait(barrier, len(partners))

    def halo(i, source, target, dev):
        return pltpu.make_async_remote_copy(
            src_ref=xbuf.at[source],
            dst_ref=xbuf.at[target],
            send_sem=halo_send.at[i],
            recv_sem=halo_recv.at[i],
            device_id=(dev,),
            device_id_type=MESH,
        )

    def along_z(k, zz, dev):
        return (
            pltpu.make_async_remote_copy(
                src_ref=coef.at[c, v, u, pl.ds(pl.multiple_of(zz * 8, 8), 8)],
                dst_ref=coef.at[c, v, u, pl.ds(pl.multiple_of(zz * 8, 8), 8)],
                send_sem=z_send.at[k, 0],
                recv_sem=z_recv.at[k, 0],
                device_id=(dev,),
                device_id_type=MESH,
            ),
            pltpu.make_async_remote_copy(
                src_ref=stage.at[zz],
                dst_ref=stage.at[zz],
                send_sem=z_send.at[k, 1],
                recv_sem=z_recv.at[k, 1],
                device_id=(dev,),
                device_id_type=MESH,
            ),
        )

    order = [4, 3, 5, 2, 6, 1, 7]
    sends = []
    for k in order:
        pair = along_z(k - 1, z, device(v, u, mod(z + k, Z)))
        for copy in pair:
            copy.start()
        sends += pair
    halo_copies = [halo(0, 1, 0, right), halo(1, 1, 2, left)]
    for copy in halo_copies:
        copy.start()
    sends += halo_copies

    def place(s, shift):
        cc = (s >> shift) & 1
        zz = (s >> (shift + 1)) & 7
        yy = (s >> (shift + 4)) & 3
        xx = (s >> (shift + 6)) & 3
        vv = jnp.where(cc == 0, xx, yy)
        uu = jnp.where(cc == 0, yy, xx)
        return cc * 128 + vv * 32 + uu * 8 + zz

    def live_of(counts, width):
        n = len(counts)
        row = iota((n, width), 0)
        cap = jnp.zeros((n, width), jnp.int32)
        for i, count in enumerate(counts):
            cap = jnp.where(row == i, count, cap)
        return iota((n, width), 1) < cap

    def slots():
        s = leaf_list[...]
        k = place(s, 3) * 8 + (s & 7)
        k = jnp.where(live_of([leaf_count[i] for i in range(8)], 48), k, -1)
        m = mid_list[...]
        km = jnp.where(iota((1, 48), 1) < mid_count[0], place(m, 0), -1)
        pad = jnp.full((16, 80), -1, jnp.int32)
        both = jnp.concatenate([k, jnp.broadcast_to(km, (8, 48))], axis=0)
        cols = jnp.transpose(jnp.concatenate([both, pad], axis=1).astype(F32))
        lanes = iota((48, 256), 1).astype(F32)
        for l in range(8):
            col = jnp.broadcast_to(cols[:48, l : l + 1], (48, 256))
            for q in range(8):
                onehot[l * 48 : (l + 1) * 48, q * 256 : (q + 1) * 256] = jnp.where(
                    lanes + (q * 256.0) == col, 1.0, 0.0
                ).astype(BF16)
        col = jnp.broadcast_to(cols[:48, 8:9], (48, 256))
        onehot2[0:48, :] = jnp.where(lanes == col, 1.0, 0.0).astype(BF16)
        wanted = jnp.where(iota((16, 32), 1) == lax.div(me, 8), top_list[...], 0)
        wanted = jnp.sum(wanted.astype(F32), axis=1, keepdims=True)
        k = iota((16, 256), 1)
        vv, uu = (k >> 5) & 3, (k >> 3) & 3
        xx = jnp.where(k < 128, vv, uu)
        yy = jnp.where(k < 128, uu, vv)
        top = ((xx * 4 + yy) * 2 + ((k & 7) >> 2)).astype(F32)
        onehot2[48:64, :] = jnp.where(
            top == jnp.broadcast_to(wanted, (16, 256)), 1.0, 0.0
        ).astype(BF16)

    slots()

    for k in order:
        zz = mod(z - k, Z)
        for copy in along_z(k - 1, zz, me):
            copy.wait_recv()
    coef[c, v, u, 64:72, :] = stage[:, 0, :]
    coef[c, v, u, 72:80, :] = stage[:, 1, :]

    def column(i, cc, vv, uu, half, dev):
        ref = coef.at[cc, vv, uu]
        if half is not None:
            ref = coef.at[cc, vv, uu, pl.ds(half * HALF, HALF)]
        return pltpu.make_async_remote_copy(
            src_ref=ref,
            dst_ref=ref,
            send_sem=col_send.at[i],
            recv_sem=col_recv.at[i],
            device_id=(dev,),
            device_id_type=MESH,
        )

    def send(i, vv, uu, half, dev):
        copy = column(i, c, vv, uu, half, dev)
        copy.start()
        sends.append(copy)

    def arrive(i, vv, uu, half):
        column(i, c, vv, uu, half, me).wait_recv()

    def second(k, uu):
        send(V1P + k, v, uu, None, dev_vp)
        send(V1M + k, v, uu, None, dev_vm)
        send(SIB + k, v, uu, None, sibling)

    u2, v2 = mod(u + 2, 4), mod(v + 2, 4)
    send(U1P, v, u, None, dev_up)
    send(U1M, v, u, None, dev_um)
    second(0, u)

    for i, (source, target) in enumerate([(1, 0), (1, 2)]):
        halo(i, target, target, me).wait_recv()
    low = iota((8, 128), 1) < 64
    xe[0, 24] = jnp.zeros((8, 128), F32)
    xe[1, 24] = jnp.zeros((8, 128), F32)
    for i in range(12):
        tile = xbuf[i // 4, :, (i % 4) * 128 : (i % 4 + 1) * 128]
        turned = pltpu.roll(tile, 64, 1)
        xe[0, 2 * i] = tile
        xe[1, 2 * i] = turned
        xe[0, 2 * i + 1] = turned
        xe[1, 2 * i + 1] = tile
    base = me * 8 - 8

    def near_pair(i):
        outs = []
        for l in (2 * i, 2 * i + 1):
            count = near_count[l]

            def pick(n, side):
                s = jnp.clip(near_list[l, n] - base, 0, 23)
                return xe[side, jnp.where(n < count, s, 24)]

            parts = [
                jnp.where(low, pick(n, 0), pick(n + 1, 1)) for n in range(0, 26, 2)
            ]
            parts.append(pick(26, 0)[:, :64])
            lhs = jnp.concatenate(parts, axis=1)
            outs.append(product(lhs, near_v[l].reshape(27 * 64, 64)))
        near_acc[:, i * 128 : (i + 1) * 128] = jnp.concatenate(outs, axis=1)

    for i in range(2):
        load_near[i].wait()
        near_pair(i)

    arrive(U1P, v, um, None)
    send(U2P, v, um, 0, dev_up)
    second(3, um)
    arrive(U1M, v, up, None)
    send(U2M, v, up, 1, dev_um)
    second(1, up)

    for i in range(2, 4):
        load_near[i].wait()
        near_pair(i)

    arrive(U2P, v, u2, 0)
    arrive(U2M, v, u2, 1)
    second(2, u2)

    load_leaf.wait()
    load_mid.wait()
    load_top.wait()

    def pack(cp):
        gap = jnp.zeros((32, 16), F32)
        blocks = []
        for l in range(8):
            first, other = (2 * cp, 2 * cp + 1) if l % 2 == 0 else (2 * cp + 1, 2 * cp)
            blocks.append(
                jnp.concatenate([leaf_v[l, first], gap, leaf_v[l, other], gap], axis=1)
            )
        hi, lo = split(jnp.transpose(jnp.concatenate(blocks, axis=0)))
        rows = pl.ds(pl.multiple_of(cp * 128, 128), 128)
        whi[rows, :] = hi
        wlo[rows, :] = lo
        block = jnp.concatenate([mid_v[2 * cp], gap, mid_v[2 * cp + 1], gap], axis=1)
        block = jnp.transpose(
            jnp.concatenate([block, jnp.zeros((96, 128), F32)], axis=0)
        )
        rest = jnp.zeros((48, 32), F32)
        top = jnp.concatenate(
            [top_v[:, 2 * cp + 1, :], rest, top_v[:, 2 * cp, :], rest], axis=0
        )
        top = jnp.concatenate(
            [jnp.zeros((128, 32), F32), top, jnp.zeros((128, 64), F32)], axis=1
        )
        hi, lo = split(block + top)
        w2hi[rows, :] = hi
        w2lo[rows, :] = lo

    lax.fori_loop(0, 8, lambda i, _: (pack(i), 0)[1], 0)

    ks = [(0, u), (3, um), (1, up), (2, u2)]
    for k, uu in ks:
        arrive(V1P + k, vm, uu, None)
        send(V2P + k, vm, uu, 0, dev_vp)
        send(SIB + 4 + k, vm, uu, None, sibling)
        arrive(V1M + k, vp, uu, None)
        send(V2M + k, vp, uu, 1, dev_vm)
        send(SIB + 8 + k, vp, uu, None, sibling)

    lax.fori_loop(8, 16, lambda i, _: (pack(i), 0)[1], 0)

    load_mdn.wait()
    load_ldn.wait()
    load_lout.wait()
    wide = []
    for l in range(8):
        pieces = [lout_v[l]]
        if l:
            pieces.insert(0, jnp.zeros((32, 64 * l), F32))
        if l < 7:
            pieces.append(jnp.zeros((32, 64 * (7 - l)), F32))
        wide.append(jnp.concatenate(pieces, axis=1))
    wide = jnp.concatenate(wide, axis=0)
    down = product(jnp.transpose(ldn_v[...].reshape(256, 32)), wide)
    down2 = product(jnp.transpose(mdn_v[0]), down)
    for rows, value in (
        (pl.ds(0, 256), wide),
        (pl.ds(256, 32), down),
        (pl.ds(288, 32), down2),
        (pl.ds(320, 64), jnp.zeros((64, 512), F32)),
    ):
        hi, lo = split(value)
        ohi[rows, :] = hi
        olo[rows, :] = lo

    def plane(cc, vv, first):
        hi, lo = split(coef[cc, vv, :, 0:64, :].reshape(256, 256))
        lanes = pl.ds(pl.multiple_of((cc * 4 + vv) * 256, 256), 256)
        rows = onehot[:, lanes]
        part = (dot(rows, hi) + dot(rows, lo)).reshape(8, 48, 256)
        if first:
            picked[:, 0:48, :] = part
        else:
            picked[:, 0:48, :] += part

    picked[:, 48:64, :] = jnp.zeros((8, 16, 256), F32)
    plane(c, v, True)
    plane(c, vm, False)
    plane(c, vp, False)

    for k, uu in ks:
        arrive(V2P + k, v2, uu, 0)
        arrive(V2M + k, v2, uu, 1)
        send(SIB + 12 + k, v2, uu, None, sibling)
    plane(c, v2, False)

    for q, vv in enumerate([u, um, up, u2]):
        for k, uu in [(0, v), (3, vm), (1, vp), (2, v2)]:
            column(SIB + 4 * q + k, 1 - c, vv, uu, None, me).wait_recv()
        plane(1 - c, vv, False)

    mid_rows = coef[:, :, :, 64:72, :].reshape(256, 256)
    top_rows = coef[:, :, :, 72:80, :].reshape(256, 256)
    hi, lo = split(mid_rows)
    rows = onehot2[0:48, :]
    mid_picked = dot(rows, hi) + dot(rows, lo)
    hi, lo = split(top_rows)
    rows = onehot2[48:64, :]
    top_picked = dot(rows, hi) + dot(rows, lo)

    turned = [
        jnp.transpose(picked[2 * i : 2 * i + 2].reshape(128, 256)) for i in range(4)
    ]
    gap = jnp.zeros((16, 256), F32)
    turned.append(
        jnp.transpose(
            jnp.concatenate([mid_picked, gap, top_picked, gap, gap, gap], axis=0)
        )
    )
    lhs = []
    for t in turned:
        even, odd = [], []
        for cp in range(16):
            a = t[16 * cp : 16 * cp + 8]
            b = pltpu.roll(t[16 * cp + 8 : 16 * cp + 16], 64, 1)
            even.append(jnp.where(low, a, b))
            odd.append(jnp.where(low, b, a))
        lhs += [jnp.concatenate(even, axis=1), jnp.concatenate(odd, axis=1)]
    far = product2(jnp.concatenate(lhs[:8], axis=0), whi[...], wlo[...])
    far = far.reshape(8, 8, 256)
    own = iota((8, 8, 256), 2) // 32 == iota((8, 8, 256), 0)
    far = jnp.sum(jnp.where(own, far, 0.0), axis=0)
    high = product2(jnp.concatenate(lhs[8:], axis=0), w2hi[...], w2lo[...])
    high = jnp.where(iota((8, 128), 1) < 32, high[:8], high[8:])
    field = jnp.concatenate([far, high], axis=1)
    out_ref[...] = near_acc[...] + product2(field, ohi[...], olo[...])

    for copy in sends:
        copy.wait_send()


def on_device(
    x_block,
    near_tiles,
    near_list,
    near_count,
    leaf_in,
    leaf_up,
    mid_up,
    leaf_tiles,
    leaf_list,
    leaf_count,
    mid_tiles,
    mid_list,
    mid_count,
    top_tiles,
    top_list,
    mid_down,
    leaf_down,
    leaf_out,
):
    smem = pl.BlockSpec(memory_space=pltpu.SMEM)
    vmem = pl.BlockSpec(memory_space=pltpu.VMEM)
    hbm = pl.BlockSpec(memory_space=pl.ANY)
    return pl.pallas_call(
        kernel,
        out_shape=jax.ShapeDtypeStruct((8, 512), F32),
        in_specs=[smem] * 4 + [vmem] * 3 + [hbm] * 11,
        out_specs=vmem,
        scratch_shapes=[
            pltpu.VMEM((3, 8, 512), F32),
            pltpu.VMEM((8, 27, 64, 64), F32),
            pltpu.VMEM((8, 32, 32, 48), F32),
            pltpu.VMEM((32, 32, 48), F32),
            pltpu.VMEM((16, 32, 32), F32),
            pltpu.VMEM((8, 32, 64), F32),
            pltpu.VMEM((8, 32, 32), F32),
            pltpu.VMEM((1, 32, 32), F32),
            pltpu.VMEM((1, 32, 32), F32),
            pltpu.VMEM((8, 32, 32), F32),
            pltpu.VMEM((8, 32, 64), F32),
            pltpu.VMEM((2, 4, 4, ROWS, 256), F32),
            pltpu.VMEM((8, 2, 256), F32),
            pltpu.VMEM((2, 25, 8, 128), F32),
            pltpu.VMEM((8, 512), F32),
            pltpu.VMEM((384, 2048), BF16),
            pltpu.VMEM((64, 256), BF16),
            pltpu.VMEM((8, 64, 256), F32),
            pltpu.VMEM((2048, 256), BF16),
            pltpu.VMEM((2048, 256), BF16),
            pltpu.VMEM((2048, 128), BF16),
            pltpu.VMEM((2048, 128), BF16),
            pltpu.VMEM((384, 512), BF16),
            pltpu.VMEM((384, 512), BF16),
            pltpu.SemaphoreType.DMA((10,)),
            pltpu.SemaphoreType.DMA((4,)),
            pltpu.SemaphoreType.DMA((2,)),
            pltpu.SemaphoreType.DMA((2,)),
            pltpu.SemaphoreType.DMA((7, 2)),
            pltpu.SemaphoreType.DMA((7, 2)),
            pltpu.SemaphoreType.DMA((COPIES,)),
            pltpu.SemaphoreType.DMA((COPIES,)),
        ],
        compiler_params=pltpu.CompilerParams(
            collective_id=0, has_side_effects=True, vmem_limit_bytes=50 * 2**20
        ),
    )(
        near_list,
        near_count,
        leaf_count,
        mid_count,
        leaf_list,
        mid_list,
        top_list.T,
        x_block,
        near_tiles,
        leaf_tiles.transpose(0, 2, 3, 1),
        mid_tiles[0].transpose(1, 2, 0),
        top_tiles,
        leaf_in.transpose(0, 2, 1),
        leaf_up,
        mid_up,
        mid_down,
        leaf_down,
        leaf_out.transpose(0, 2, 1),
    )


def solution(mesh):
    placed = (
        P(None, "cluster"),
        P("cluster", None, None, None),
        P("cluster", None),
        P("cluster"),
        P("cluster", None, None),
        P("cluster", None, None),
        P("cluster", None, None),
        P("cluster", None, None, None),
        P("cluster", None),
        P("cluster"),
        P("cluster", None, None, None),
        P("cluster", None),
        P("cluster"),
        P(),
        P(),
        P("cluster", None, None),
        P("cluster", None, None),
        P("cluster", None, None),
    )
    return jax.shard_map(
        on_device, mesh=mesh, in_specs=placed, out_specs=P(None, "cluster"), check_vma=False
    )
```

```python
import functools

import jax
import jax.numpy as jnp
from jax import lax
from jax.experimental import pallas as pl
from jax.experimental.pallas import tpu as pltpu
from jax.sharding import PartitionSpec as P

F32 = jnp.float32
BF16 = jnp.bfloat16
MESH = pl.DeviceIdType.MESH

X, Y, Z = 4, 4, 8
ROWS = 80

HALF = ROWS // 2
U_ID, V_ID, W_ID = 0, 3, 15
FORWARDED = 3
COPIES = 24


def mod(a, n):
    return lax.rem(a + n, n)


def stacked(a):
    hi = a.astype(BF16).astype(F32)
    return jnp.concatenate([hi, a - hi], axis=0).astype(BF16)


def split(b):
    hi = b.astype(BF16)
    return hi, (b - hi.astype(F32)).astype(BF16)


def dot(a, b):
    return jnp.dot(a, b, preferred_element_type=F32)


def product2(a, hi, lo):
    both = stacked(a)
    out = dot(both, hi) + dot(both, lo)
    half = out.shape[0] // 2
    return out[:half] + out[half:]


def product(a, b):
    return product2(a, *split(b))


def iota(shape, dim):
    return lax.broadcasted_iota(jnp.int32, shape, dim)


def kernel(
    near_list_hbm,
    near_count_hbm,
    leaf_count_hbm,
    mid_count_hbm,
    leaf_list_hbm,
    mid_list_hbm,
    top_list_hbm,
    x_hbm,
    near_hbm,
    leaf_hbm,
    mid_hbm,
    top_hbm,
    lin_hbm,
    lup_hbm,
    mup_hbm,
    mdn_hbm,
    ldn_hbm,
    lout_hbm,
    out_ref,
    near_list,
    near_count,
    leaf_count,
    mid_count,
    leaf_list,
    mid_list,
    top_list,
    xbuf,
    near_v,
    leaf_v,
    mid_v,
    top_v,
    lin_v,
    lup_v,
    mup_v,
    mdn_v,
    ldn_v,
    lout_v,
    coef,
    stage,
    xe,
    near_acc,
    onehot,
    onehot2,
    picked,
    whi,
    wlo,
    w2hi,
    w2lo,
    ohi,
    olo,
    load_sem,
    near_sem,
    halo_send,
    halo_recv,
    z_send,
    z_recv,
    col_send,
    col_recv,
    wanted_rows,
    swap_send,
    swap_recv,
):
    me = lax.axis_index("cluster")
    c = lax.rem(me, 2)
    z = lax.rem(lax.div(me, 2), Z)
    y = lax.rem(lax.div(me, 2 * Z), Y)
    x = lax.div(me, 2 * Z * Y)
    v = x + c * (y - x)
    u = y + c * (x - y)

    def device(vv, uu, zz):
        xx = vv + c * (uu - vv)
        yy = uu + c * (vv - uu)
        return ((xx * Y + yy) * Z + zz) * 2 + c

    sibling = me + 1 - 2 * c
    right = mod(me + 1, 256)
    left = mod(me - 1, 256)

    def load(i, source, target):
        copy = pltpu.make_async_copy(source, target, load_sem.at[i])
        copy.start()
        return copy

    load_x = load(0, x_hbm, xbuf.at[1])
    load_lin = load(1, lin_hbm, lin_v)
    load_lup = load(2, lup_hbm, lup_v)
    load_mup = load(3, mup_hbm, mup_v)
    barrier = pltpu.get_barrier_semaphore()
    partners = [device(v, u, mod(z + k, Z)) for k in range(1, Z)]
    up, um = mod(u + 1, 4), mod(u - 1, 4)
    vp, vm = mod(v + 1, 4), mod(v - 1, 4)
    dev_up, dev_um = device(v, up, z), device(v, um, z)
    dev_vp, dev_vm = device(vp, u, z), device(vm, u, z)
    u2, v2 = mod(u + 2, 4), mod(v + 2, 4)
    dev_u2, dev_v2 = device(v, u2, z), device(v2, u, z)
    partners += [dev_up, dev_um, dev_u2, dev_vp, dev_vm, dev_v2, sibling, right, left]
    for partner in partners:
        pl.semaphore_signal(barrier, inc=1, device_id=(partner,), device_id_type=MESH)

    load_x.wait()
    load_lin.wait()
    load_lup.wait()
    load_mup.wait()
    zeros64 = jnp.zeros((32, 64), F32)
    r_parts = []
    for i in range(4):
        block = jnp.concatenate(
            [
                jnp.concatenate([lin_v[2 * i], zeros64], axis=1),
                jnp.concatenate([zeros64, lin_v[2 * i + 1]], axis=1),
            ],
            axis=0,
        )
        hi, lo = split(block)
        both = stacked(xbuf[1, :, i * 128 : (i + 1) * 128])
        nt = functools.partial(
            lax.dot_general,
            dimension_numbers=(((1,), (1,)), ((), ())),
            preferred_element_type=F32,
        )
        part = nt(both, hi) + nt(both, lo)
        r_parts.append(part[:8] + part[8:])
    r = jnp.concatenate(r_parts, axis=1)
    lup = lup_v[...].reshape(256, 32)
    both_up = jnp.concatenate([lup, product(lup, mup_v[0])], axis=1)
    spread = (iota((32, 256), 0) % 8 == iota((32, 256), 1) % 8).astype(BF16)
    same = iota((32, 256), 0) == iota((32, 256), 1) // 8

    def flat(a):
        n = a.shape[1] // 32
        if n % 4:
            a = jnp.concatenate([a, jnp.zeros((8, 32 * (4 - n % 4)), F32)], axis=1)
        hi = a.astype(BF16).astype(F32)
        rest = a - hi
        mid = rest.astype(BF16).astype(F32)
        parts = jnp.concatenate([hi, mid, rest - mid, jnp.zeros_like(a)], axis=0)
        rows = dot(jnp.transpose(parts).astype(BF16), spread)[: 32 * n]
        return jnp.sum(jnp.where(same[None], rows.reshape(n, 32, 256), 0.0), axis=1)

    my_rows = pl.ds(pl.multiple_of(z * 8, 8), 8)
    coef[c, v, u, my_rows, :] = flat(r)

    pl.semaphore_wait(barrier, len(partners))

    def halo(i, source, target, dev):
        return pltpu.make_async_remote_copy(
            src_ref=xbuf.at[source],
            dst_ref=xbuf.at[target],
            send_sem=halo_send.at[i],
            recv_sem=halo_recv.at[i],
            device_id=(dev,),
            device_id_type=MESH,
        )

    def along_z(k, zz, dev):
        return (
            pltpu.make_async_remote_copy(
                src_ref=coef.at[c, v, u, pl.ds(pl.multiple_of(zz * 8, 8), 8)],
                dst_ref=coef.at[c, v, u, pl.ds(pl.multiple_of(zz * 8, 8), 8)],
                send_sem=z_send.at[k, 0],
                recv_sem=z_recv.at[k, 0],
                device_id=(dev,),
                device_id_type=MESH,
            ),
            pltpu.make_async_remote_copy(
                src_ref=stage.at[zz],
                dst_ref=stage.at[zz],
                send_sem=z_send.at[k, 1],
                recv_sem=z_recv.at[k, 1],
                device_id=(dev,),
                device_id_type=MESH,
            ),
        )

    order = [4, 3, 5, 2, 6, 1, 7]
    sends = []
    for k in order:
        copy = along_z(k - 1, z, device(v, u, mod(z + k, Z)))[0]
        copy.start()
        sends.append(copy)
    stage[z] = flat(product(r, both_up))
    for k in order:
        copy = along_z(k - 1, z, device(v, u, mod(z + k, Z)))[1]
        copy.start()
        sends.append(copy)
    load_lists = [
        load(10, leaf_count_hbm, leaf_count),
        load(11, mid_count_hbm, mid_count),
        load(12, leaf_list_hbm, leaf_list),
        load(13, mid_list_hbm, mid_list),
        load(14, top_list_hbm, top_list),
        load(15, near_list_hbm, near_list),
        load(16, near_count_hbm, near_count),
    ]
    load_near = []
    for i in range(4):
        copy = pltpu.make_async_copy(
            near_hbm.at[pl.ds(2 * i, 2)], near_v.at[pl.ds(2 * i, 2)], near_sem.at[i]
        )
        copy.start()
        load_near.append(copy)
    load_leaf = load(4, leaf_hbm, leaf_v)
    load_mid = load(5, mid_hbm, mid_v)
    load_top = load(6, top_hbm.at[lax.div(me, 8)], top_v)
    load_mdn = load(7, mdn_hbm, mdn_v)
    load_ldn = load(8, ldn_hbm, ldn_v)
    load_lout = load(9, lout_hbm, lout_v)

    halo_copies = [halo(0, 1, 0, right), halo(1, 1, 2, left)]
    for copy in halo_copies:
        copy.start()
    sends += halo_copies

    def place(s, shift):
        cc = (s >> shift) & 1
        zz = (s >> (shift + 1)) & 7
        yy = (s >> (shift + 4)) & 3
        xx = (s >> (shift + 6)) & 3
        vv = jnp.where(cc == 0, xx, yy)
        uu = jnp.where(cc == 0, yy, xx)
        return cc, uu * 32 + vv * 8 + zz

    def live_of(counts, width):
        n = len(counts)
        row = iota((n, width), 0)
        cap = jnp.zeros((n, width), jnp.int32)
        for i, count in enumerate(counts):
            cap = jnp.where(row == i, count, cap)
        return iota((n, width), 1) < cap

    def slots():
        s = leaf_list[...]
        cc, k = place(s, 3)
        k = cc * 1024 + k * 8 + (s & 7)
        k = jnp.where(live_of([leaf_count[i] for i in range(8)], 48), k, -1)
        cc, km = place(mid_list[...], 0)
        km = cc * 256 + (km >> 3) * 16 + (km & 7)
        km = jnp.where(iota((1, 48), 1) < mid_count[0, 0], km, -1)
        both = jnp.concatenate([k, jnp.broadcast_to(km, (8, 48))], axis=0)
        pad = jnp.full((16, 80), -1, jnp.int32)
        wanted_rows[0] = jnp.concatenate([both, pad], axis=1).astype(F32)

    def list_copy():
        return pltpu.make_async_remote_copy(
            src_ref=wanted_rows.at[0],
            dst_ref=wanted_rows.at[1],
            send_sem=swap_send.at[0],
            recv_sem=swap_recv.at[0],
            device_id=(sibling,),
            device_id_type=MESH,
        )

    def one_hot(side):
        cols = jnp.transpose(wanted_rows[side])
        start = (c * 1024).astype(F32)
        lanes = iota((48, 256), 1).astype(F32)
        for l in range(8):
            col = jnp.broadcast_to(cols[:48, l : l + 1], (48, 256)) - start
            rows = slice(side * 384 + l * 48, side * 384 + (l + 1) * 48)
            for t in range(4):
                onehot[rows, t * 256 : (t + 1) * 256] = jnp.where(
                    lanes + (t * 256.0) == col, 1.0, 0.0
                ).astype(BF16)
        start = (c * 256).astype(F32)
        col = jnp.broadcast_to(cols[:48, 8:9], (48, 256)) - start
        onehot2[side * 64 : side * 64 + 48, :] = jnp.where(
            lanes == col, 1.0, 0.0
        ).astype(BF16)
        wanted = jnp.where(iota((16, 32), 1) == lax.div(me, 8), top_list[...], 0)
        wanted = jnp.sum(wanted.astype(F32), axis=1, keepdims=True)
        k = iota((16, 256), 1)
        uu, vv = (k >> 6) & 3, (k >> 4) & 3
        xx = vv + c * (uu - vv)
        yy = uu + c * (vv - uu)
        top = (xx * 4 + yy) * 2 + ((k & 7) >> 2)
        top = jnp.where((k & 8) == 8, top, -1).astype(F32)
        onehot2[side * 64 + 48 : side * 64 + 64, :] = jnp.where(
            top == jnp.broadcast_to(wanted, (16, 256)), 1.0, 0.0
        ).astype(BF16)

    for copy in load_lists:
        copy.wait()
    slots()
    list_copy().start()
    one_hot(0)

    for k in order:
        zz = mod(z - k, Z)
        for copy in along_z(k - 1, zz, me):
            copy.wait_recv()
    coef[c, v, u, 64:72, :] = stage[:, 0, :]
    coef[c, v, u, 72:80, :] = stage[:, 1, :]

    def column(i, vv, uu, dev, half=None):
        ref = coef.at[c, vv, uu]
        if half is not None:
            ref = coef.at[c, vv, uu, pl.ds(half * HALF, HALF)]
        return pltpu.make_async_remote_copy(
            src_ref=ref,
            dst_ref=ref,
            send_sem=col_send.at[i],
            recv_sem=col_recv.at[i],
            device_id=(dev,),
            device_id_type=MESH,
        )

    def send(i, vv, uu, dev, half=None):
        copy = column(i, vv, uu, dev, half)
        copy.start()
        sends.append(copy)

    def along_v(k, uu):
        if k >= FORWARDED:
            send(V_ID + 3 * k, v, uu, dev_v2)
        send(V_ID + 3 * k + 1, v, uu, dev_vp)
        send(V_ID + 3 * k + 2, v, uu, dev_vm)

    send(U_ID, v, u, dev_u2)
    send(U_ID + 1, v, u, dev_up)
    send(U_ID + 2, v, u, dev_um)
    along_v(0, u)
    list_copy().wait_recv()
    one_hot(1)

    for i, (source, target) in enumerate([(1, 0), (1, 2)]):
        halo(i, target, target, me).wait_recv()
    low = iota((8, 128), 1) < 64
    xe[0, 24] = jnp.zeros((8, 128), F32)
    xe[1, 24] = jnp.zeros((8, 128), F32)
    for i in range(12):
        tile = xbuf[i // 4, :, (i % 4) * 128 : (i % 4 + 1) * 128]
        turned = pltpu.roll(tile, 64, 1)
        xe[0, 2 * i] = tile
        xe[1, 2 * i] = turned
        xe[0, 2 * i + 1] = turned
        xe[1, 2 * i + 1] = tile
    base = me * 8 - 8

    def near_pair(i):
        outs = []
        for l in (2 * i, 2 * i + 1):
            count = near_count[l]

            def pick(n, side):
                s = jnp.clip(near_list[l, n] - base, 0, 23)
                return xe[side, jnp.where(n < count, s, 24)]

            parts = [
                jnp.where(low, pick(n, 0), pick(n + 1, 1)) for n in range(0, 26, 2)
            ]
            parts.append(pick(26, 0)[:, :64])
            lhs = jnp.concatenate(parts, axis=1)
            outs.append(product(lhs, near_v[l].reshape(27 * 64, 64)))
        near_acc[:, i * 128 : (i + 1) * 128] = jnp.concatenate(outs, axis=1)

    for i in range(4):
        load_near[i].wait()
        near_pair(i)

    column(U_ID + 1, v, um, me).wait_recv()
    along_v(1, um)
    column(U_ID + 2, v, up, me).wait_recv()
    along_v(2, up)
    column(U_ID, v, u2, me).wait_recv()
    along_v(3, u2)

    load_leaf.wait()
    load_mid.wait()
    load_top.wait()

    def pack(cp):
        gap = jnp.zeros((32, 16), F32)
        blocks = []
        for l in range(8):
            first, other = (2 * cp, 2 * cp + 1) if l % 2 == 0 else (2 * cp + 1, 2 * cp)
            blocks.append(
                jnp.concatenate([leaf_v[l, first], gap, leaf_v[l, other], gap], axis=1)
            )
        hi, lo = split(jnp.transpose(jnp.concatenate(blocks, axis=0)))
        rows = pl.ds(pl.multiple_of(cp * 128, 128), 128)
        whi[rows, :] = hi
        wlo[rows, :] = lo
        block = jnp.concatenate([mid_v[2 * cp], gap, mid_v[2 * cp + 1], gap], axis=1)
        block = jnp.transpose(
            jnp.concatenate([block, jnp.zeros((96, 128), F32)], axis=0)
        )
        rest = jnp.zeros((48, 32), F32)
        top = jnp.concatenate(
            [top_v[:, 2 * cp + 1, :], rest, top_v[:, 2 * cp, :], rest], axis=0
        )
        top = jnp.concatenate(
            [jnp.zeros((128, 32), F32), top, jnp.zeros((128, 64), F32)], axis=1
        )
        hi, lo = split(block + top)
        w2hi[rows, :] = hi
        w2lo[rows, :] = lo

    lax.fori_loop(0, 16, lambda i, _: (pack(i), 0)[1], 0)

    load_mdn.wait()
    load_ldn.wait()
    load_lout.wait()
    wide = []
    for l in range(8):
        pieces = [lout_v[l]]
        if l:
            pieces.insert(0, jnp.zeros((32, 64 * l), F32))
        if l < 7:
            pieces.append(jnp.zeros((32, 64 * (7 - l)), F32))
        wide.append(jnp.concatenate(pieces, axis=1))
    wide = jnp.concatenate(wide, axis=0)
    down = product(jnp.transpose(ldn_v[...].reshape(256, 32)), wide)
    down2 = product(jnp.transpose(mdn_v[0]), down)
    for rows, value in (
        (pl.ds(0, 256), wide),
        (pl.ds(256, 32), down),
        (pl.ds(288, 32), down2),
        (pl.ds(320, 64), jnp.zeros((64, 512), F32)),
    ):
        hi, lo = split(value)
        ohi[rows, :] = hi
        olo[rows, :] = lo

    def plane(uu, side, first):
        hi, lo = split(coef[c, :, uu, 0:64, :].reshape(256, 256))
        lanes = pl.ds(pl.multiple_of(uu * 256, 256), 256)
        rows = onehot[side * 384 : (side + 1) * 384, lanes]
        part = dot(rows, hi) + dot(rows, lo)
        if first:
            picked[side, 0:384, :] = part
        else:
            picked[side, 0:384, :] += part

    def upper(side):
        hi, lo = split(coef[c, :, :, 64:80, :].swapaxes(0, 1).reshape(256, 256))
        rows = onehot2[side * 64 : (side + 1) * 64, :]
        picked[side, 384:448, :] = dot(rows, hi) + dot(rows, lo)

    def swap():
        return pltpu.make_async_remote_copy(
            src_ref=picked.at[1],
            dst_ref=picked.at[2],
            send_sem=swap_send.at[1],
            recv_sem=swap_recv.at[1],
            device_id=(sibling,),
            device_id_type=MESH,
        )

    for k, uu in enumerate([u, um, up, u2]):
        column(V_ID + 3 * k + 1, vm, uu, me).wait_recv()
        if k < FORWARDED:
            send(W_ID + 2 * k, vm, uu, dev_vp, 0)
        column(V_ID + 3 * k + 2, vp, uu, me).wait_recv()
        if k < FORWARDED:
            send(W_ID + 2 * k + 1, vp, uu, dev_vm, 1)
    for k, uu in enumerate([u, um, up, u2]):
        if k < FORWARDED:
            column(W_ID + 2 * k, v2, uu, me, 0).wait_recv()
            column(W_ID + 2 * k + 1, v2, uu, me, 1).wait_recv()
        else:
            column(V_ID + 3 * k, v2, uu, me).wait_recv()
        if k < 3:
            plane(uu, 1, k == 0)
            plane(uu, 0, k == 0)
    upper(1)
    plane(u2, 1, False)
    swap().start()
    upper(0)
    plane(u2, 0, False)
    swap().wait_recv()
    total = picked[0] + picked[2]

    gap = jnp.zeros((16, 256), F32)
    turned = []
    for i in range(5):
        first, second = total[96 * i : 96 * i + 48], total[96 * i + 48 : 96 * i + 96]
        if i == 4:
            second = jnp.concatenate([second, gap, gap], axis=0)
        turned.append(jnp.transpose(jnp.concatenate([first, gap, second, gap], axis=0)))
    lhs = []
    for t in turned:
        even, odd = [], []
        for cp in range(16):
            a = t[16 * cp : 16 * cp + 8]
            b = pltpu.roll(t[16 * cp + 8 : 16 * cp + 16], 64, 1)
            even.append(jnp.where(low, a, b))
            odd.append(jnp.where(low, b, a))
        lhs += [jnp.concatenate(even, axis=1), jnp.concatenate(odd, axis=1)]
    far = product2(jnp.concatenate(lhs[:8], axis=0), whi[...], wlo[...])
    far = far.reshape(8, 8, 256)
    own = iota((8, 8, 256), 2) // 32 == iota((8, 8, 256), 0)
    far = jnp.sum(jnp.where(own, far, 0.0), axis=0)
    high = product2(jnp.concatenate(lhs[8:], axis=0), w2hi[...], w2lo[...])
    high = jnp.where(iota((8, 128), 1) < 32, high[:8], high[8:])
    field = jnp.concatenate([far, high], axis=1)
    out_ref[...] = near_acc[...] + product2(field, ohi[...], olo[...])

    for copy in sends + [list_copy(), swap()]:
        copy.wait_send()


def on_device(
    x_block,
    near_tiles,
    near_list,
    near_count,
    leaf_in,
    leaf_up,
    mid_up,
    leaf_tiles,
    leaf_list,
    leaf_count,
    mid_tiles,
    mid_list,
    mid_count,
    top_tiles,
    top_list,
    mid_down,
    leaf_down,
    leaf_out,
):
    vmem = pl.BlockSpec(memory_space=pltpu.VMEM)
    hbm = pl.BlockSpec(memory_space=pltpu.HBM)
    return pl.pallas_call(
        kernel,
        out_shape=pltpu.VMEM((8, 512), F32),
        in_specs=[hbm] * 18,
        out_specs=vmem,
        scratch_shapes=[
            pltpu.SMEM((8, 27), jnp.int32),
            pltpu.SMEM((8,), jnp.int32),
            pltpu.SMEM((8,), jnp.int32),
            pltpu.SMEM((1, 1), jnp.int32),
            pltpu.VMEM((8, 48), jnp.int32),
            pltpu.VMEM((1, 48), jnp.int32),
            pltpu.VMEM((16, 32), jnp.int32),
            pltpu.VMEM((3, 8, 512), F32),
            pltpu.VMEM((8, 27, 64, 64), F32),
            pltpu.VMEM((8, 32, 32, 48), F32),
            pltpu.VMEM((32, 32, 48), F32),
            pltpu.VMEM((16, 32, 32), F32),
            pltpu.VMEM((8, 32, 64), F32),
            pltpu.VMEM((8, 32, 32), F32),
            pltpu.VMEM((1, 32, 32), F32),
            pltpu.VMEM((1, 32, 32), F32),
            pltpu.VMEM((8, 32, 32), F32),
            pltpu.VMEM((8, 32, 64), F32),
            pltpu.VMEM((2, 4, 4, ROWS, 256), F32),
            pltpu.VMEM((8, 2, 256), F32),
            pltpu.VMEM((2, 25, 8, 128), F32),
            pltpu.VMEM((8, 512), F32),
            pltpu.VMEM((768, 1024), BF16),
            pltpu.VMEM((128, 256), BF16),
            pltpu.VMEM((3, 448, 256), F32),
            pltpu.VMEM((2048, 256), BF16),
            pltpu.VMEM((2048, 256), BF16),
            pltpu.VMEM((2048, 128), BF16),
            pltpu.VMEM((2048, 128), BF16),
            pltpu.VMEM((384, 512), BF16),
            pltpu.VMEM((384, 512), BF16),
            pltpu.SemaphoreType.DMA((17,)),
            pltpu.SemaphoreType.DMA((4,)),
            pltpu.SemaphoreType.DMA((2,)),
            pltpu.SemaphoreType.DMA((2,)),
            pltpu.SemaphoreType.DMA((7, 2)),
            pltpu.SemaphoreType.DMA((7, 2)),
            pltpu.SemaphoreType.DMA((COPIES,)),
            pltpu.SemaphoreType.DMA((COPIES,)),
            pltpu.VMEM((2, 16, 128), F32),
            pltpu.SemaphoreType.DMA((2,)),
            pltpu.SemaphoreType.DMA((2,)),
        ],
        compiler_params=pltpu.CompilerParams(
            collective_id=0, has_side_effects=True, vmem_limit_bytes=60 * 2**20
        ),
    )(
        near_list,
        near_count,
        leaf_count,
        mid_count.reshape(1, 1),
        leaf_list,
        mid_list,
        top_list.T,
        x_block,
        near_tiles,
        leaf_tiles.transpose(0, 2, 3, 1),
        mid_tiles[0].transpose(1, 2, 0),
        top_tiles,
        leaf_in.transpose(0, 2, 1),
        leaf_up,
        mid_up,
        mid_down,
        leaf_down,
        leaf_out.transpose(0, 2, 1),
    )


def solution(mesh):
    placed = (
        P(None, "cluster"),
        P("cluster", None, None, None),
        P("cluster", None),
        P("cluster"),
        P("cluster", None, None),
        P("cluster", None, None),
        P("cluster", None, None),
        P("cluster", None, None, None),
        P("cluster", None),
        P("cluster"),
        P("cluster", None, None, None),
        P("cluster", None),
        P("cluster"),
        P(),
        P(),
        P("cluster", None, None),
        P("cluster", None, None),
        P("cluster", None, None),
    )
    return jax.shard_map(
        on_device, mesh=mesh, in_specs=placed, out_specs=P(None, "cluster"), check_vma=False
    )
```

```python
import functools

import jax
import jax.numpy as jnp
from jax import lax
from jax.experimental import pallas as pl
from jax.experimental.pallas import tpu as pltpu
from jax.sharding import PartitionSpec as P

F32 = jnp.float32
BF16 = jnp.bfloat16
MESH = pl.DeviceIdType.MESH

X, Y, Z = 4, 4, 8
ROWS = 80

HALF = ROWS // 2
U_ID, V_ID, W_ID = 0, 3, 15
FORWARDED = 0
COPIES = 24


def mod(a, n):
    return lax.rem(a + n, n)


def stacked(a):
    hi = a.astype(BF16).astype(F32)
    return jnp.concatenate([hi, a - hi], axis=0).astype(BF16)


def split(b):
    hi = b.astype(BF16)
    return hi, (b - hi.astype(F32)).astype(BF16)


def dot(a, b):
    return jnp.dot(a, b, preferred_element_type=F32)


def product2(a, hi, lo):
    both = stacked(a)
    out = dot(both, hi) + dot(both, lo)
    half = out.shape[0] // 2
    return out[:half] + out[half:]


def product(a, b):
    return product2(a, *split(b))


def iota(shape, dim):
    return lax.broadcasted_iota(jnp.int32, shape, dim)


def kernel(
    near_list_hbm,
    near_count_hbm,
    leaf_count_hbm,
    mid_count_hbm,
    leaf_list_hbm,
    mid_list_hbm,
    top_list_hbm,
    x_hbm,
    near_hbm,
    leaf_hbm,
    mid_hbm,
    top_hbm,
    lin_hbm,
    lup_hbm,
    mup_hbm,
    mdn_hbm,
    ldn_hbm,
    lout_hbm,
    out_ref,
    near_list,
    near_count,
    leaf_count,
    mid_count,
    leaf_list,
    mid_list,
    top_list,
    xbuf,
    near_v,
    leaf_v,
    mid_v,
    top_v,
    lin_v,
    lup_v,
    mup_v,
    mdn_v,
    ldn_v,
    lout_v,
    coef,
    stage,
    xe,
    near_acc,
    onehot,
    onehot2,
    picked,
    whi,
    wlo,
    w2hi,
    w2lo,
    ohi,
    olo,
    load_sem,
    near_sem,
    halo_send,
    halo_recv,
    z_send,
    z_recv,
    col_send,
    col_recv,
    wanted_rows,
    swap_send,
    swap_recv,
):
    me = lax.axis_index("cluster")
    c = lax.rem(me, 2)
    z = lax.rem(lax.div(me, 2), Z)
    y = lax.rem(lax.div(me, 2 * Z), Y)
    x = lax.div(me, 2 * Z * Y)
    v = x + c * (y - x)
    u = y + c * (x - y)

    def device(vv, uu, zz):
        xx = vv + c * (uu - vv)
        yy = uu + c * (vv - uu)
        return ((xx * Y + yy) * Z + zz) * 2 + c

    sibling = me + 1 - 2 * c
    right = mod(me + 1, 256)
    left = mod(me - 1, 256)

    def load(i, source, target):
        copy = pltpu.make_async_copy(source, target, load_sem.at[i])
        copy.start()
        return copy

    load_x = load(0, x_hbm, xbuf.at[1])
    load_lin = load(1, lin_hbm, lin_v)
    load_lup = load(2, lup_hbm, lup_v)
    load_mup = load(3, mup_hbm, mup_v)
    barrier = pltpu.get_barrier_semaphore()
    partners = [device(v, u, mod(z + k, Z)) for k in range(1, Z)]
    up, um = mod(u + 1, 4), mod(u - 1, 4)
    vp, vm = mod(v + 1, 4), mod(v - 1, 4)
    dev_up, dev_um = device(v, up, z), device(v, um, z)
    dev_vp, dev_vm = device(vp, u, z), device(vm, u, z)
    u2, v2 = mod(u + 2, 4), mod(v + 2, 4)
    dev_u2, dev_v2 = device(v, u2, z), device(v2, u, z)
    partners += [dev_up, dev_um, dev_u2, dev_vp, dev_vm, dev_v2, sibling, right, left]
    for partner in partners:
        pl.semaphore_signal(barrier, inc=1, device_id=(partner,), device_id_type=MESH)

    load_x.wait()
    load_lin.wait()
    load_lup.wait()
    load_mup.wait()
    zeros64 = jnp.zeros((32, 64), F32)
    r_parts = []
    for i in range(4):
        block = jnp.concatenate(
            [
                jnp.concatenate([lin_v[2 * i], zeros64], axis=1),
                jnp.concatenate([zeros64, lin_v[2 * i + 1]], axis=1),
            ],
            axis=0,
        )
        hi, lo = split(block)
        both = stacked(xbuf[1, :, i * 128 : (i + 1) * 128])
        nt = functools.partial(
            lax.dot_general,
            dimension_numbers=(((1,), (1,)), ((), ())),
            preferred_element_type=F32,
        )
        part = nt(both, hi) + nt(both, lo)
        r_parts.append(part[:8] + part[8:])
    r = jnp.concatenate(r_parts, axis=1)
    lup = lup_v[...].reshape(256, 32)
    both_up = jnp.concatenate([lup, product(lup, mup_v[0])], axis=1)
    spread = (iota((32, 256), 0) % 8 == iota((32, 256), 1) % 8).astype(BF16)
    same = iota((32, 256), 0) == iota((32, 256), 1) // 8

    def flat(a):
        n = a.shape[1] // 32
        if n % 4:
            a = jnp.concatenate([a, jnp.zeros((8, 32 * (4 - n % 4)), F32)], axis=1)
        hi = a.astype(BF16).astype(F32)
        rest = a - hi
        mid = rest.astype(BF16).astype(F32)
        parts = jnp.concatenate([hi, mid, rest - mid, jnp.zeros_like(a)], axis=0)
        rows = dot(jnp.transpose(parts).astype(BF16), spread)[: 32 * n]
        return jnp.sum(jnp.where(same[None], rows.reshape(n, 32, 256), 0.0), axis=1)

    my_rows = pl.ds(pl.multiple_of(z * 8, 8), 8)
    coef[c, v, u, my_rows, :] = flat(r)

    pl.semaphore_wait(barrier, len(partners))

    def halo(i, source, target, dev):
        return pltpu.make_async_remote_copy(
            src_ref=xbuf.at[source],
            dst_ref=xbuf.at[target],
            send_sem=halo_send.at[i],
            recv_sem=halo_recv.at[i],
            device_id=(dev,),
            device_id_type=MESH,
        )

    def along_z(k, zz, dev):
        return (
            pltpu.make_async_remote_copy(
                src_ref=coef.at[c, v, u, pl.ds(pl.multiple_of(zz * 8, 8), 8)],
                dst_ref=coef.at[c, v, u, pl.ds(pl.multiple_of(zz * 8, 8), 8)],
                send_sem=z_send.at[k, 0],
                recv_sem=z_recv.at[k, 0],
                device_id=(dev,),
                device_id_type=MESH,
            ),
            pltpu.make_async_remote_copy(
                src_ref=stage.at[zz],
                dst_ref=stage.at[zz],
                send_sem=z_send.at[k, 1],
                recv_sem=z_recv.at[k, 1],
                device_id=(dev,),
                device_id_type=MESH,
            ),
        )

    order = [4, 3, 5, 2, 6, 1, 7]
    sends = []
    for k in order:
        copy = along_z(k - 1, z, device(v, u, mod(z + k, Z)))[0]
        copy.start()
        sends.append(copy)
    stage[z] = flat(product(r, both_up))
    for k in order:
        copy = along_z(k - 1, z, device(v, u, mod(z + k, Z)))[1]
        copy.start()
        sends.append(copy)
    load_lists = [
        load(10, leaf_count_hbm, leaf_count),
        load(11, mid_count_hbm, mid_count),
        load(12, leaf_list_hbm, leaf_list),
        load(13, mid_list_hbm, mid_list),
        load(14, top_list_hbm, top_list),
        load(15, near_list_hbm, near_list),
        load(16, near_count_hbm, near_count),
    ]
    load_near = []
    for i in range(4):
        copy = pltpu.make_async_copy(
            near_hbm.at[pl.ds(2 * i, 2)], near_v.at[pl.ds(2 * i, 2)], near_sem.at[i]
        )
        copy.start()
        load_near.append(copy)
    load_leaf = load(4, leaf_hbm, leaf_v)
    load_mid = load(5, mid_hbm, mid_v)
    load_top = load(6, top_hbm.at[lax.div(me, 8)], top_v)
    load_mdn = load(7, mdn_hbm, mdn_v)
    load_ldn = load(8, ldn_hbm, ldn_v)
    load_lout = load(9, lout_hbm, lout_v)

    halo_copies = [halo(0, 1, 0, right), halo(1, 1, 2, left)]
    for copy in halo_copies:
        copy.start()
    sends += halo_copies

    def place(s, shift):
        cc = (s >> shift) & 1
        zz = (s >> (shift + 1)) & 7
        yy = (s >> (shift + 4)) & 3
        xx = (s >> (shift + 6)) & 3
        vv = jnp.where(cc == 0, xx, yy)
        uu = jnp.where(cc == 0, yy, xx)
        return cc, uu * 32 + vv * 8 + zz

    def live_of(counts, width):
        n = len(counts)
        row = iota((n, width), 0)
        cap = jnp.zeros((n, width), jnp.int32)
        for i, count in enumerate(counts):
            cap = jnp.where(row == i, count, cap)
        return iota((n, width), 1) < cap

    def slots():
        s = leaf_list[...]
        cc, k = place(s, 3)
        k = cc * 1024 + k * 8 + (s & 7)
        k = jnp.where(live_of([leaf_count[i] for i in range(8)], 48), k, -1)
        cc, km = place(mid_list[...], 0)
        km = cc * 256 + (km >> 3) * 16 + (km & 7)
        km = jnp.where(iota((1, 48), 1) < mid_count[0, 0], km, -1)
        both = jnp.concatenate([k, jnp.broadcast_to(km, (8, 48))], axis=0)
        pad = jnp.full((16, 80), -1, jnp.int32)
        wanted_rows[0] = jnp.concatenate([both, pad], axis=1).astype(F32)

    def list_copy():
        return pltpu.make_async_remote_copy(
            src_ref=wanted_rows.at[0],
            dst_ref=wanted_rows.at[1],
            send_sem=swap_send.at[0],
            recv_sem=swap_recv.at[0],
            device_id=(sibling,),
            device_id_type=MESH,
        )

    def one_hot(side):
        cols = jnp.transpose(wanted_rows[side])
        start = (c * 1024).astype(F32)
        lanes = iota((48, 256), 1).astype(F32)
        for l in range(8):
            col = jnp.broadcast_to(cols[:48, l : l + 1], (48, 256)) - start
            rows = slice(side * 384 + l * 48, side * 384 + (l + 1) * 48)
            for t in range(4):
                onehot[rows, t * 256 : (t + 1) * 256] = jnp.where(
                    lanes + (t * 256.0) == col, 1.0, 0.0
                ).astype(BF16)
        start = (c * 256).astype(F32)
        col = jnp.broadcast_to(cols[:48, 8:9], (48, 256)) - start
        onehot2[side * 64 : side * 64 + 48, :] = jnp.where(
            lanes == col, 1.0, 0.0
        ).astype(BF16)
        wanted = jnp.where(iota((16, 32), 1) == lax.div(me, 8), top_list[...], 0)
        wanted = jnp.sum(wanted.astype(F32), axis=1, keepdims=True)
        k = iota((16, 256), 1)
        uu, vv = (k >> 6) & 3, (k >> 4) & 3
        xx = vv + c * (uu - vv)
        yy = uu + c * (vv - uu)
        top = (xx * 4 + yy) * 2 + ((k & 7) >> 2)
        top = jnp.where((k & 8) == 8, top, -1).astype(F32)
        onehot2[side * 64 + 48 : side * 64 + 64, :] = jnp.where(
            top == jnp.broadcast_to(wanted, (16, 256)), 1.0, 0.0
        ).astype(BF16)

    for copy in load_lists:
        copy.wait()
    slots()
    list_copy().start()
    one_hot(0)

    for k in order:
        zz = mod(z - k, Z)
        for copy in along_z(k - 1, zz, me):
            copy.wait_recv()
    coef[c, v, u, 64:72, :] = stage[:, 0, :]
    coef[c, v, u, 72:80, :] = stage[:, 1, :]

    def column(i, vv, uu, dev, half=None):
        ref = coef.at[c, vv, uu]
        if half is not None:
            ref = coef.at[c, vv, uu, pl.ds(half * HALF, HALF)]
        return pltpu.make_async_remote_copy(
            src_ref=ref,
            dst_ref=ref,
            send_sem=col_send.at[i],
            recv_sem=col_recv.at[i],
            device_id=(dev,),
            device_id_type=MESH,
        )

    def send(i, vv, uu, dev, half=None):
        copy = column(i, vv, uu, dev, half)
        copy.start()
        sends.append(copy)

    def along_v(k, uu):
        send(V_ID + 3 * k + 1, v, uu, dev_vp)
        send(V_ID + 3 * k + 2, v, uu, dev_vm)
        if k >= FORWARDED:
            send(V_ID + 3 * k, v, uu, dev_v2)

    send(U_ID + 1, v, u, dev_up)
    send(U_ID + 2, v, u, dev_um)
    send(U_ID, v, u, dev_u2)
    list_copy().wait_recv()
    one_hot(1)

    for i, (source, target) in enumerate([(1, 0), (1, 2)]):
        halo(i, target, target, me).wait_recv()
    low = iota((8, 128), 1) < 64
    xe[0, 24] = jnp.zeros((8, 128), F32)
    xe[1, 24] = jnp.zeros((8, 128), F32)
    for i in range(12):
        tile = xbuf[i // 4, :, (i % 4) * 128 : (i % 4 + 1) * 128]
        turned = pltpu.roll(tile, 64, 1)
        xe[0, 2 * i] = tile
        xe[1, 2 * i] = turned
        xe[0, 2 * i + 1] = turned
        xe[1, 2 * i + 1] = tile
    base = me * 8 - 8

    def near_pair(i):
        outs = []
        for l in (2 * i, 2 * i + 1):
            count = near_count[l]

            def pick(n, side):
                s = jnp.clip(near_list[l, n] - base, 0, 23)
                return xe[side, jnp.where(n < count, s, 24)]

            parts = [
                jnp.where(low, pick(n, 0), pick(n + 1, 1)) for n in range(0, 26, 2)
            ]
            parts.append(pick(26, 0)[:, :64])
            lhs = jnp.concatenate(parts, axis=1)
            outs.append(product(lhs, near_v[l].reshape(27 * 64, 64)))
        near_acc[:, i * 128 : (i + 1) * 128] = jnp.concatenate(outs, axis=1)

    for i in range(4):
        load_near[i].wait()
        near_pair(i)
        if i == 3:
            along_v(0, u)

    column(U_ID + 1, v, um, me).wait_recv()
    along_v(1, um)
    column(U_ID + 2, v, up, me).wait_recv()
    along_v(2, up)
    column(U_ID, v, u2, me).wait_recv()
    along_v(3, u2)

    load_leaf.wait()
    load_mid.wait()
    load_top.wait()

    def pack(cp):
        gap = jnp.zeros((32, 16), F32)
        blocks = []
        for l in range(8):
            first, other = (2 * cp, 2 * cp + 1) if l % 2 == 0 else (2 * cp + 1, 2 * cp)
            blocks.append(
                jnp.concatenate([leaf_v[l, first], gap, leaf_v[l, other], gap], axis=1)
            )
        hi, lo = split(jnp.transpose(jnp.concatenate(blocks, axis=0)))
        rows = pl.ds(pl.multiple_of(cp * 128, 128), 128)
        whi[rows, :] = hi
        wlo[rows, :] = lo
        block = jnp.concatenate([mid_v[2 * cp], gap, mid_v[2 * cp + 1], gap], axis=1)
        block = jnp.transpose(
            jnp.concatenate([block, jnp.zeros((96, 128), F32)], axis=0)
        )
        rest = jnp.zeros((48, 32), F32)
        top = jnp.concatenate(
            [top_v[:, 2 * cp + 1, :], rest, top_v[:, 2 * cp, :], rest], axis=0
        )
        top = jnp.concatenate(
            [jnp.zeros((128, 32), F32), top, jnp.zeros((128, 64), F32)], axis=1
        )
        hi, lo = split(block + top)
        w2hi[rows, :] = hi
        w2lo[rows, :] = lo

    lax.fori_loop(0, 16, lambda i, _: (pack(i), 0)[1], 0)

    load_mdn.wait()
    load_ldn.wait()
    load_lout.wait()
    wide = []
    for l in range(8):
        pieces = [lout_v[l]]
        if l:
            pieces.insert(0, jnp.zeros((32, 64 * l), F32))
        if l < 7:
            pieces.append(jnp.zeros((32, 64 * (7 - l)), F32))
        wide.append(jnp.concatenate(pieces, axis=1))
    wide = jnp.concatenate(wide, axis=0)
    down = product(jnp.transpose(ldn_v[...].reshape(256, 32)), wide)
    down2 = product(jnp.transpose(mdn_v[0]), down)
    for rows, value in (
        (pl.ds(0, 256), wide),
        (pl.ds(256, 32), down),
        (pl.ds(288, 32), down2),
        (pl.ds(320, 64), jnp.zeros((64, 512), F32)),
    ):
        hi, lo = split(value)
        ohi[rows, :] = hi
        olo[rows, :] = lo

    def plane(uu, side, first):
        hi, lo = split(coef[c, :, uu, 0:64, :].reshape(256, 256))
        lanes = pl.ds(pl.multiple_of(uu * 256, 256), 256)
        rows = onehot[side * 384 : (side + 1) * 384, lanes]
        part = dot(rows, hi) + dot(rows, lo)
        if first:
            picked[side, 0:384, :] = part
        else:
            picked[side, 0:384, :] += part

    def upper(side):
        hi, lo = split(coef[c, :, :, 64:80, :].swapaxes(0, 1).reshape(256, 256))
        rows = onehot2[side * 64 : (side + 1) * 64, :]
        picked[side, 384:448, :] = dot(rows, hi) + dot(rows, lo)

    def swap():
        return pltpu.make_async_remote_copy(
            src_ref=picked.at[1],
            dst_ref=picked.at[2],
            send_sem=swap_send.at[1],
            recv_sem=swap_recv.at[1],
            device_id=(sibling,),
            device_id_type=MESH,
        )

    for k, uu in enumerate([u, um, up, u2]):
        column(V_ID + 3 * k + 1, vm, uu, me).wait_recv()
        if k < FORWARDED:
            send(W_ID + 2 * k, vm, uu, dev_vp, 0)
        column(V_ID + 3 * k + 2, vp, uu, me).wait_recv()
        if k < FORWARDED:
            send(W_ID + 2 * k + 1, vp, uu, dev_vm, 1)
    for k, uu in enumerate([u, um, up, u2]):
        if k < FORWARDED:
            column(W_ID + 2 * k, v2, uu, me, 0).wait_recv()
            column(W_ID + 2 * k + 1, v2, uu, me, 1).wait_recv()
        else:
            column(V_ID + 3 * k, v2, uu, me).wait_recv()
        if k < 3:
            plane(uu, 1, k == 0)
            plane(uu, 0, k == 0)
    upper(1)
    plane(u2, 1, False)
    swap().start()
    upper(0)
    plane(u2, 0, False)
    swap().wait_recv()
    total = picked[0] + picked[2]

    gap = jnp.zeros((16, 256), F32)
    turned = []
    for i in range(5):
        first, second = total[96 * i : 96 * i + 48], total[96 * i + 48 : 96 * i + 96]
        if i == 4:
            second = jnp.concatenate([second, gap, gap], axis=0)
        turned.append(jnp.transpose(jnp.concatenate([first, gap, second, gap], axis=0)))
    lhs = []
    for t in turned:
        even, odd = [], []
        for cp in range(16):
            a = t[16 * cp : 16 * cp + 8]
            b = pltpu.roll(t[16 * cp + 8 : 16 * cp + 16], 64, 1)
            even.append(jnp.where(low, a, b))
            odd.append(jnp.where(low, b, a))
        lhs += [jnp.concatenate(even, axis=1), jnp.concatenate(odd, axis=1)]
    far = product2(jnp.concatenate(lhs[:8], axis=0), whi[...], wlo[...])
    far = far.reshape(8, 8, 256)
    own = iota((8, 8, 256), 2) // 32 == iota((8, 8, 256), 0)
    far = jnp.sum(jnp.where(own, far, 0.0), axis=0)
    high = product2(jnp.concatenate(lhs[8:], axis=0), w2hi[...], w2lo[...])
    high = jnp.where(iota((8, 128), 1) < 32, high[:8], high[8:])
    field = jnp.concatenate([far, high], axis=1)
    out_ref[...] = near_acc[...] + product2(field, ohi[...], olo[...])

    for copy in sends + [list_copy(), swap()]:
        copy.wait_send()


def on_device(
    x_block,
    near_tiles,
    near_list,
    near_count,
    leaf_in,
    leaf_up,
    mid_up,
    leaf_tiles,
    leaf_list,
    leaf_count,
    mid_tiles,
    mid_list,
    mid_count,
    top_tiles,
    top_list,
    mid_down,
    leaf_down,
    leaf_out,
):
    vmem = pl.BlockSpec(memory_space=pltpu.VMEM)
    hbm = pl.BlockSpec(memory_space=pltpu.HBM)
    return pl.pallas_call(
        kernel,
        out_shape=pltpu.VMEM((8, 512), F32),
        in_specs=[hbm] * 18,
        out_specs=vmem,
        scratch_shapes=[
            pltpu.SMEM((8, 27), jnp.int32),
            pltpu.SMEM((8,), jnp.int32),
            pltpu.SMEM((8,), jnp.int32),
            pltpu.SMEM((1, 1), jnp.int32),
            pltpu.VMEM((8, 48), jnp.int32),
            pltpu.VMEM((1, 48), jnp.int32),
            pltpu.VMEM((16, 32), jnp.int32),
            pltpu.VMEM((3, 8, 512), F32),
            pltpu.VMEM((8, 27, 64, 64), F32),
            pltpu.VMEM((8, 32, 32, 48), F32),
            pltpu.VMEM((32, 32, 48), F32),
            pltpu.VMEM((16, 32, 32), F32),
            pltpu.VMEM((8, 32, 64), F32),
            pltpu.VMEM((8, 32, 32), F32),
            pltpu.VMEM((1, 32, 32), F32),
            pltpu.VMEM((1, 32, 32), F32),
            pltpu.VMEM((8, 32, 32), F32),
            pltpu.VMEM((8, 32, 64), F32),
            pltpu.VMEM((2, 4, 4, ROWS, 256), F32),
            pltpu.VMEM((8, 2, 256), F32),
            pltpu.VMEM((2, 25, 8, 128), F32),
            pltpu.VMEM((8, 512), F32),
            pltpu.VMEM((768, 1024), BF16),
            pltpu.VMEM((128, 256), BF16),
            pltpu.VMEM((3, 448, 256), F32),
            pltpu.VMEM((2048, 256), BF16),
            pltpu.VMEM((2048, 256), BF16),
            pltpu.VMEM((2048, 128), BF16),
            pltpu.VMEM((2048, 128), BF16),
            pltpu.VMEM((384, 512), BF16),
            pltpu.VMEM((384, 512), BF16),
            pltpu.SemaphoreType.DMA((17,)),
            pltpu.SemaphoreType.DMA((4,)),
            pltpu.SemaphoreType.DMA((2,)),
            pltpu.SemaphoreType.DMA((2,)),
            pltpu.SemaphoreType.DMA((7, 2)),
            pltpu.SemaphoreType.DMA((7, 2)),
            pltpu.SemaphoreType.DMA((COPIES,)),
            pltpu.SemaphoreType.DMA((COPIES,)),
            pltpu.VMEM((2, 16, 128), F32),
            pltpu.SemaphoreType.DMA((2,)),
            pltpu.SemaphoreType.DMA((2,)),
        ],
        compiler_params=pltpu.CompilerParams(
            collective_id=0, has_side_effects=True, vmem_limit_bytes=60 * 2**20
        ),
    )(
        near_list,
        near_count,
        leaf_count,
        mid_count.reshape(1, 1),
        leaf_list,
        mid_list,
        top_list.T,
        x_block,
        near_tiles,
        leaf_tiles.transpose(0, 2, 3, 1),
        mid_tiles[0].transpose(1, 2, 0),
        top_tiles,
        leaf_in.transpose(0, 2, 1),
        leaf_up,
        mid_up,
        mid_down,
        leaf_down,
        leaf_out.transpose(0, 2, 1),
    )


def solution(mesh):
    placed = (
        P(None, "cluster"),
        P("cluster", None, None, None),
        P("cluster", None),
        P("cluster"),
        P("cluster", None, None),
        P("cluster", None, None),
        P("cluster", None, None),
        P("cluster", None, None, None),
        P("cluster", None),
        P("cluster"),
        P("cluster", None, None, None),
        P("cluster", None),
        P("cluster"),
        P(),
        P(),
        P("cluster", None, None),
        P("cluster", None, None),
        P("cluster", None, None),
    )
    return jax.shard_map(
        on_device, mesh=mesh, in_specs=placed, out_specs=P(None, "cluster"), check_vma=False
    )
```

```python
import functools

import jax
import jax.numpy as jnp
from jax import lax
from jax.experimental import pallas as pl
from jax.experimental.pallas import tpu as pltpu
from jax.sharding import PartitionSpec as P

F32 = jnp.float32
BF16 = jnp.bfloat16
MESH = pl.DeviceIdType.MESH

X, Y, Z = 4, 4, 8
ROWS = 80

HALF = ROWS // 2
REL_U, REL_V, REL_SIB, REL_RIGHT, REL_LEFT = 8, 11, 14, 15, 16
RELATIONS = 17
U_ID, V_ID, W_ID = 0, 3, 15
FORWARDED = 0
COPIES = 24


def mod(a, n):
    return lax.rem(a + n, n)


def stacked(a):
    hi = a.astype(BF16).astype(F32)
    return jnp.concatenate([hi, a - hi], axis=0).astype(BF16)


def split(b):
    hi = b.astype(BF16)
    return hi, (b - hi.astype(F32)).astype(BF16)


def dot(a, b):
    return jnp.dot(a, b, preferred_element_type=F32)


def product2(a, hi, lo):
    both = stacked(a)
    out = dot(both, hi) + dot(both, lo)
    half = out.shape[0] // 2
    return out[:half] + out[half:]


def product(a, b):
    return product2(a, *split(b))


def iota(shape, dim):
    return lax.broadcasted_iota(jnp.int32, shape, dim)


def kernel(
    near_list_hbm,
    near_count_hbm,
    leaf_count_hbm,
    mid_count_hbm,
    leaf_list_hbm,
    mid_list_hbm,
    top_list_hbm,
    x_hbm,
    near_hbm,
    leaf_hbm,
    mid_hbm,
    top_hbm,
    lin_hbm,
    lup_hbm,
    mup_hbm,
    mdn_hbm,
    ldn_hbm,
    lout_hbm,
    out_ref,
    near_list,
    near_count,
    leaf_count,
    mid_count,
    leaf_list,
    mid_list,
    top_list,
    xbuf,
    near_v,
    leaf_v,
    mid_v,
    top_v,
    lin_v,
    lup_v,
    mup_v,
    mdn_v,
    ldn_v,
    lout_v,
    coef,
    stage,
    xe,
    near_acc,
    onehot,
    onehot2,
    picked,
    whi,
    wlo,
    w2hi,
    w2lo,
    ohi,
    olo,
    load_sem,
    near_sem,
    halo_send,
    halo_recv,
    z_send,
    z_recv,
    col_send,
    col_recv,
    wanted_rows,
    swap_send,
    swap_recv,
    ready_sem,
):
    me = lax.axis_index("cluster")
    c = lax.rem(me, 2)
    z = lax.rem(lax.div(me, 2), Z)
    y = lax.rem(lax.div(me, 2 * Z), Y)
    x = lax.div(me, 2 * Z * Y)
    v = x + c * (y - x)
    u = y + c * (x - y)

    def device(vv, uu, zz):
        xx = vv + c * (uu - vv)
        yy = uu + c * (vv - uu)
        return ((xx * Y + yy) * Z + zz) * 2 + c

    sibling = me + 1 - 2 * c
    right = mod(me + 1, 256)
    left = mod(me - 1, 256)

    def load(i, source, target):
        copy = pltpu.make_async_copy(source, target, load_sem.at[i])
        copy.start()
        return copy

    load_x = load(0, x_hbm, xbuf.at[1])
    load_lin = load(1, lin_hbm, lin_v)
    load_lup = load(2, lup_hbm, lup_v)
    load_mup = load(3, mup_hbm, mup_v)
    up, um, u2 = mod(u + 1, 4), mod(u - 1, 4), mod(u + 2, 4)
    vp, vm, v2 = mod(v + 1, 4), mod(v - 1, 4), mod(v + 2, 4)
    dev_up, dev_um, dev_u2 = device(v, up, z), device(v, um, z), device(v, u2, z)
    dev_vp, dev_vm, dev_v2 = device(vp, u, z), device(vm, u, z), device(v2, u, z)

    def rank(dev):
        xx = lax.div(dev, 2 * Z * Y)
        yy = lax.rem(lax.div(dev, 2 * Z), Y)
        zz = lax.rem(lax.div(dev, 2), Z)
        return ((zz * Y + yy) * X + xx) * 2 + lax.rem(dev, 2)

    mine = rank(me)
    relations = [
        (REL_U, dev_u2, REL_U),
        (REL_U + 1, dev_up, REL_U + 2),
        (REL_U + 2, dev_um, REL_U + 1),
        (REL_V, dev_v2, REL_V),
        (REL_V + 1, dev_vp, REL_V + 2),
        (REL_V + 2, dev_vm, REL_V + 1),
        (REL_SIB, sibling, REL_SIB),
        (REL_RIGHT, right, REL_LEFT),
        (REL_LEFT, left, REL_RIGHT),
    ]
    relations += [(k, device(v, u, mod(z + k, Z)), Z - k) for k in range(1, Z)]
    relations = [(i, dev, rank(dev), back) for i, dev, back in relations]
    barrier = pltpu.get_barrier_semaphore()
    greetings = jnp.int32(0)
    for _, dev, theirs, _ in relations:
        greetings += (theirs < mine).astype(jnp.int32)

        @pl.when(mine < theirs)
        def _():
            pl.semaphore_signal(barrier, inc=1, device_id=(dev,), device_id_type=MESH)

    def ready(relation):
        for i, _, theirs, _ in relations:
            if i == relation:

                @pl.when(mine < theirs)
                def _():
                    pl.semaphore_wait(ready_sem.at[i], 1)

    load_x.wait()
    load_lin.wait()
    load_lup.wait()
    load_mup.wait()
    zeros64 = jnp.zeros((32, 64), F32)
    r_parts = []
    for i in range(4):
        block = jnp.concatenate(
            [
                jnp.concatenate([lin_v[2 * i], zeros64], axis=1),
                jnp.concatenate([zeros64, lin_v[2 * i + 1]], axis=1),
            ],
            axis=0,
        )
        hi, lo = split(block)
        both = stacked(xbuf[1, :, i * 128 : (i + 1) * 128])
        nt = functools.partial(
            lax.dot_general,
            dimension_numbers=(((1,), (1,)), ((), ())),
            preferred_element_type=F32,
        )
        part = nt(both, hi) + nt(both, lo)
        r_parts.append(part[:8] + part[8:])
    r = jnp.concatenate(r_parts, axis=1)
    lup = lup_v[...].reshape(256, 32)
    both_up = jnp.concatenate([lup, product(lup, mup_v[0])], axis=1)
    spread = (iota((32, 256), 0) % 8 == iota((32, 256), 1) % 8).astype(BF16)
    same = iota((32, 256), 0) == iota((32, 256), 1) // 8

    def flat(a):
        n = a.shape[1] // 32
        if n % 4:
            a = jnp.concatenate([a, jnp.zeros((8, 32 * (4 - n % 4)), F32)], axis=1)
        hi = a.astype(BF16).astype(F32)
        rest = a - hi
        mid = rest.astype(BF16).astype(F32)
        parts = jnp.concatenate([hi, mid, rest - mid, jnp.zeros_like(a)], axis=0)
        rows = dot(jnp.transpose(parts).astype(BF16), spread)[: 32 * n]
        return jnp.sum(jnp.where(same[None], rows.reshape(n, 32, 256), 0.0), axis=1)

    my_rows = pl.ds(pl.multiple_of(z * 8, 8), 8)
    coef[c, v, u, my_rows, :] = flat(r)

    @pl.when(greetings > 0)
    def _():
        pl.semaphore_wait(barrier, greetings)

    for _, dev, theirs, back in relations:

        @pl.when(theirs < mine)
        def _():
            pl.semaphore_signal(
                ready_sem.at[back], inc=1, device_id=(dev,), device_id_type=MESH
            )

    def halo(i, source, target, dev):
        return pltpu.make_async_remote_copy(
            src_ref=xbuf.at[source],
            dst_ref=xbuf.at[target],
            send_sem=halo_send.at[i],
            recv_sem=halo_recv.at[i],
            device_id=(dev,),
            device_id_type=MESH,
        )

    def along_z(k, zz, dev):
        return (
            pltpu.make_async_remote_copy(
                src_ref=coef.at[c, v, u, pl.ds(pl.multiple_of(zz * 8, 8), 8)],
                dst_ref=coef.at[c, v, u, pl.ds(pl.multiple_of(zz * 8, 8), 8)],
                send_sem=z_send.at[k, 0],
                recv_sem=z_recv.at[k, 0],
                device_id=(dev,),
                device_id_type=MESH,
            ),
            pltpu.make_async_remote_copy(
                src_ref=stage.at[zz],
                dst_ref=stage.at[zz],
                send_sem=z_send.at[k, 1],
                recv_sem=z_recv.at[k, 1],
                device_id=(dev,),
                device_id_type=MESH,
            ),
        )

    halo_to = ((right, rank(right)), (left, rank(left)))
    for i, (dev, theirs) in enumerate(halo_to):

        @pl.when(theirs < mine)
        def _():
            halo(i, 1, 2 * i, dev).start()

    def to_plane(zz):
        k = mod(zz - z, Z)

        @pl.when(zz > z)
        def _():
            pl.semaphore_wait(ready_sem.at[k], 1)

        @pl.when(zz != z)
        def _():
            for copy in along_z(k, z, device(v, u, zz)):
                copy.start()

    def from_plane(zz):
        @pl.when(zz != z)
        def _():
            for copy in along_z(mod(z - zz, Z), zz, me):
                copy.wait_recv()

    stage[z] = flat(product(r, both_up))
    sends = []
    for zz in range(Z):
        to_plane(zz)
    load_lists = [
        load(10, leaf_count_hbm, leaf_count),
        load(11, mid_count_hbm, mid_count),
        load(12, leaf_list_hbm, leaf_list),
        load(13, mid_list_hbm, mid_list),
        load(14, top_list_hbm, top_list),
        load(15, near_list_hbm, near_list),
        load(16, near_count_hbm, near_count),
    ]
    load_near = []
    for i in range(4):
        copy = pltpu.make_async_copy(
            near_hbm.at[pl.ds(2 * i, 2)], near_v.at[pl.ds(2 * i, 2)], near_sem.at[i]
        )
        copy.start()
        load_near.append(copy)
    load_leaf = load(4, leaf_hbm, leaf_v)
    load_mid = load(5, mid_hbm, mid_v)
    load_top = load(6, top_hbm.at[lax.div(me, 8)], top_v)
    load_mdn = load(7, mdn_hbm, mdn_v)
    load_ldn = load(8, ldn_hbm, ldn_v)
    load_lout = load(9, lout_hbm, lout_v)

    def place(s, shift):
        cc = (s >> shift) & 1
        zz = (s >> (shift + 1)) & 7
        yy = (s >> (shift + 4)) & 3
        xx = (s >> (shift + 6)) & 3
        vv = jnp.where(cc == 0, xx, yy)
        uu = jnp.where(cc == 0, yy, xx)
        return cc, uu * 32 + vv * 8 + zz

    def live_of(counts, width):
        n = len(counts)
        row = iota((n, width), 0)
        cap = jnp.zeros((n, width), jnp.int32)
        for i, count in enumerate(counts):
            cap = jnp.where(row == i, count, cap)
        return iota((n, width), 1) < cap

    def slots():
        s = leaf_list[...]
        cc, k = place(s, 3)
        k = cc * 1024 + k * 8 + (s & 7)
        k = jnp.where(live_of([leaf_count[i] for i in range(8)], 48), k, -1)
        cc, km = place(mid_list[...], 0)
        km = cc * 256 + (km >> 3) * 16 + (km & 7)
        km = jnp.where(iota((1, 48), 1) < mid_count[0, 0], km, -1)
        both = jnp.concatenate([k, jnp.broadcast_to(km, (8, 48))], axis=0)
        pad = jnp.full((16, 80), -1, jnp.int32)
        wanted_rows[0] = jnp.concatenate([both, pad], axis=1).astype(F32)

    def list_copy():
        return pltpu.make_async_remote_copy(
            src_ref=wanted_rows.at[0],
            dst_ref=wanted_rows.at[1],
            send_sem=swap_send.at[0],
            recv_sem=swap_recv.at[0],
            device_id=(sibling,),
            device_id_type=MESH,
        )

    def one_hot(side):
        cols = jnp.transpose(wanted_rows[side])
        start = (c * 1024).astype(F32)
        lanes = iota((48, 256), 1).astype(F32)
        for l in range(8):
            col = jnp.broadcast_to(cols[:48, l : l + 1], (48, 256)) - start
            rows = slice(side * 384 + l * 48, side * 384 + (l + 1) * 48)
            for t in range(4):
                onehot[rows, t * 256 : (t + 1) * 256] = jnp.where(
                    lanes + (t * 256.0) == col, 1.0, 0.0
                ).astype(BF16)
        start = (c * 256).astype(F32)
        col = jnp.broadcast_to(cols[:48, 8:9], (48, 256)) - start
        onehot2[side * 64 : side * 64 + 48, :] = jnp.where(
            lanes == col, 1.0, 0.0
        ).astype(BF16)
        wanted = jnp.where(iota((16, 32), 1) == lax.div(me, 8), top_list[...], 0)
        wanted = jnp.sum(wanted.astype(F32), axis=1, keepdims=True)
        k = iota((16, 256), 1)
        uu, vv = (k >> 6) & 3, (k >> 4) & 3
        xx = vv + c * (uu - vv)
        yy = uu + c * (vv - uu)
        top = (xx * 4 + yy) * 2 + ((k & 7) >> 2)
        top = jnp.where((k & 8) == 8, top, -1).astype(F32)
        onehot2[side * 64 + 48 : side * 64 + 64, :] = jnp.where(
            top == jnp.broadcast_to(wanted, (16, 256)), 1.0, 0.0
        ).astype(BF16)

    for copy in load_lists:
        copy.wait()
    slots()
    ready(REL_SIB)
    list_copy().start()
    one_hot(0)
    for i, (dev, theirs) in enumerate(halo_to):

        @pl.when(mine < theirs)
        def _():
            pl.semaphore_wait(ready_sem.at[REL_RIGHT + i], 1)
            halo(i, 1, 2 * i, dev).start()

    for zz in range(Z):
        from_plane(zz)
    coef[c, v, u, 64:72, :] = stage[:, 0, :]
    coef[c, v, u, 72:80, :] = stage[:, 1, :]

    def column(i, vv, uu, dev, half=None):
        ref = coef.at[c, vv, uu]
        if half is not None:
            ref = coef.at[c, vv, uu, pl.ds(half * HALF, HALF)]
        return pltpu.make_async_remote_copy(
            src_ref=ref,
            dst_ref=ref,
            send_sem=col_send.at[i],
            recv_sem=col_recv.at[i],
            device_id=(dev,),
            device_id_type=MESH,
        )

    def send(i, vv, uu, dev, half=None):
        copy = column(i, vv, uu, dev, half)
        copy.start()
        sends.append(copy)

    def along_v(k, uu):
        send(V_ID + 3 * k + 1, v, uu, dev_vp)
        send(V_ID + 3 * k + 2, v, uu, dev_vm)
        if k >= FORWARDED:
            send(V_ID + 3 * k, v, uu, dev_v2)

    for i in range(3):
        ready(REL_U + i)
    send(U_ID + 1, v, u, dev_up)
    send(U_ID + 2, v, u, dev_um)
    send(U_ID, v, u, dev_u2)
    list_copy().wait_recv()
    one_hot(1)

    for i, (source, target) in enumerate([(1, 0), (1, 2)]):
        halo(i, target, target, me).wait_recv()
    low = iota((8, 128), 1) < 64
    xe[0, 24] = jnp.zeros((8, 128), F32)
    xe[1, 24] = jnp.zeros((8, 128), F32)
    for i in range(12):
        tile = xbuf[i // 4, :, (i % 4) * 128 : (i % 4 + 1) * 128]
        turned = pltpu.roll(tile, 64, 1)
        xe[0, 2 * i] = tile
        xe[1, 2 * i] = turned
        xe[0, 2 * i + 1] = turned
        xe[1, 2 * i + 1] = tile
    base = me * 8 - 8

    def near_pair(i):
        outs = []
        for l in (2 * i, 2 * i + 1):
            count = near_count[l]

            def pick(n, side):
                s = jnp.clip(near_list[l, n] - base, 0, 23)
                return xe[side, jnp.where(n < count, s, 24)]

            parts = [
                jnp.where(low, pick(n, 0), pick(n + 1, 1)) for n in range(0, 26, 2)
            ]
            parts.append(pick(26, 0)[:, :64])
            lhs = jnp.concatenate(parts, axis=1)
            outs.append(product(lhs, near_v[l].reshape(27 * 64, 64)))
        near_acc[:, i * 128 : (i + 1) * 128] = jnp.concatenate(outs, axis=1)

    for i in range(4):
        load_near[i].wait()
        near_pair(i)

    for i in range(3):
        ready(REL_V + i)
    along_v(0, u)
    column(U_ID + 1, v, um, me).wait_recv()
    along_v(1, um)
    column(U_ID + 2, v, up, me).wait_recv()
    along_v(2, up)
    column(U_ID, v, u2, me).wait_recv()
    along_v(3, u2)

    load_leaf.wait()
    load_mid.wait()
    load_top.wait()

    def pack(cp):
        gap = jnp.zeros((32, 16), F32)
        blocks = []
        for l in range(8):
            first, other = (2 * cp, 2 * cp + 1) if l % 2 == 0 else (2 * cp + 1, 2 * cp)
            blocks.append(
                jnp.concatenate([leaf_v[l, first], gap, leaf_v[l, other], gap], axis=1)
            )
        hi, lo = split(jnp.transpose(jnp.concatenate(blocks, axis=0)))
        rows = pl.ds(pl.multiple_of(cp * 128, 128), 128)
        whi[rows, :] = hi
        wlo[rows, :] = lo
        block = jnp.concatenate([mid_v[2 * cp], gap, mid_v[2 * cp + 1], gap], axis=1)
        block = jnp.transpose(
            jnp.concatenate([block, jnp.zeros((96, 128), F32)], axis=0)
        )
        rest = jnp.zeros((48, 32), F32)
        top = jnp.concatenate(
            [top_v[:, 2 * cp + 1, :], rest, top_v[:, 2 * cp, :], rest], axis=0
        )
        top = jnp.concatenate(
            [jnp.zeros((128, 32), F32), top, jnp.zeros((128, 64), F32)], axis=1
        )
        hi, lo = split(block + top)
        w2hi[rows, :] = hi
        w2lo[rows, :] = lo

    lax.fori_loop(0, 16, lambda i, _: (pack(i), 0)[1], 0)

    load_mdn.wait()
    load_ldn.wait()
    load_lout.wait()
    wide = []
    for l in range(8):
        pieces = [lout_v[l]]
        if l:
            pieces.insert(0, jnp.zeros((32, 64 * l), F32))
        if l < 7:
            pieces.append(jnp.zeros((32, 64 * (7 - l)), F32))
        wide.append(jnp.concatenate(pieces, axis=1))
    wide = jnp.concatenate(wide, axis=0)
    down = product(jnp.transpose(ldn_v[...].reshape(256, 32)), wide)
    down2 = product(jnp.transpose(mdn_v[0]), down)
    for rows, value in (
        (pl.ds(0, 256), wide),
        (pl.ds(256, 32), down),
        (pl.ds(288, 32), down2),
        (pl.ds(320, 64), jnp.zeros((64, 512), F32)),
    ):
        hi, lo = split(value)
        ohi[rows, :] = hi
        olo[rows, :] = lo

    def plane(uu, side, first):
        hi, lo = split(coef[c, :, uu, 0:64, :].reshape(256, 256))
        lanes = pl.ds(pl.multiple_of(uu * 256, 256), 256)
        rows = onehot[side * 384 : (side + 1) * 384, lanes]
        part = dot(rows, hi) + dot(rows, lo)
        if first:
            picked[side, 0:384, :] = part
        else:
            picked[side, 0:384, :] += part

    def upper(side):
        hi, lo = split(coef[c, :, :, 64:80, :].swapaxes(0, 1).reshape(256, 256))
        rows = onehot2[side * 64 : (side + 1) * 64, :]
        picked[side, 384:448, :] = dot(rows, hi) + dot(rows, lo)

    def swap():
        return pltpu.make_async_remote_copy(
            src_ref=picked.at[1],
            dst_ref=picked.at[2],
            send_sem=swap_send.at[1],
            recv_sem=swap_recv.at[1],
            device_id=(sibling,),
            device_id_type=MESH,
        )

    for k, uu in enumerate([u, um, up, u2]):
        column(V_ID + 3 * k + 1, vm, uu, me).wait_recv()
        if k < FORWARDED:
            send(W_ID + 2 * k, vm, uu, dev_vp, 0)
        column(V_ID + 3 * k + 2, vp, uu, me).wait_recv()
        if k < FORWARDED:
            send(W_ID + 2 * k + 1, vp, uu, dev_vm, 1)
    for k, uu in enumerate([u, um, up, u2]):
        if k < FORWARDED:
            column(W_ID + 2 * k, v2, uu, me, 0).wait_recv()
            column(W_ID + 2 * k + 1, v2, uu, me, 1).wait_recv()
        else:
            column(V_ID + 3 * k, v2, uu, me).wait_recv()
        if k < 3:
            plane(uu, 1, k == 0)
            plane(uu, 0, k == 0)
    upper(1)
    plane(u2, 1, False)
    swap().start()
    upper(0)
    plane(u2, 0, False)
    swap().wait_recv()
    total = picked[0] + picked[2]

    gap = jnp.zeros((16, 256), F32)
    turned = []
    for i in range(5):
        first, second = total[96 * i : 96 * i + 48], total[96 * i + 48 : 96 * i + 96]
        if i == 4:
            second = jnp.concatenate([second, gap, gap], axis=0)
        turned.append(jnp.transpose(jnp.concatenate([first, gap, second, gap], axis=0)))
    lhs = []
    for t in turned:
        even, odd = [], []
        for cp in range(16):
            a = t[16 * cp : 16 * cp + 8]
            b = pltpu.roll(t[16 * cp + 8 : 16 * cp + 16], 64, 1)
            even.append(jnp.where(low, a, b))
            odd.append(jnp.where(low, b, a))
        lhs += [jnp.concatenate(even, axis=1), jnp.concatenate(odd, axis=1)]
    far = product2(jnp.concatenate(lhs[:8], axis=0), whi[...], wlo[...])
    far = far.reshape(8, 8, 256)
    own = iota((8, 8, 256), 2) // 32 == iota((8, 8, 256), 0)
    far = jnp.sum(jnp.where(own, far, 0.0), axis=0)
    high = product2(jnp.concatenate(lhs[8:], axis=0), w2hi[...], w2lo[...])
    high = jnp.where(iota((8, 128), 1) < 32, high[:8], high[8:])
    field = jnp.concatenate([far, high], axis=1)
    out_ref[...] = near_acc[...] + product2(field, ohi[...], olo[...])

    for copy in sends + [list_copy(), swap()]:
        copy.wait_send()
    for i in range(2):
        halo(i, 1, 2 * i, me).wait_send()
    for k in range(1, Z):
        for copy in along_z(k, z, me):
            copy.wait_send()


def on_device(
    x_block,
    near_tiles,
    near_list,
    near_count,
    leaf_in,
    leaf_up,
    mid_up,
    leaf_tiles,
    leaf_list,
    leaf_count,
    mid_tiles,
    mid_list,
    mid_count,
    top_tiles,
    top_list,
    mid_down,
    leaf_down,
    leaf_out,
):
    vmem = pl.BlockSpec(memory_space=pltpu.VMEM)
    hbm = pl.BlockSpec(memory_space=pltpu.HBM)
    return pl.pallas_call(
        kernel,
        out_shape=pltpu.VMEM((8, 512), F32),
        in_specs=[hbm] * 18,
        out_specs=vmem,
        scratch_shapes=[
            pltpu.SMEM((8, 27), jnp.int32),
            pltpu.SMEM((8,), jnp.int32),
            pltpu.SMEM((8,), jnp.int32),
            pltpu.SMEM((1, 1), jnp.int32),
            pltpu.VMEM((8, 48), jnp.int32),
            pltpu.VMEM((1, 48), jnp.int32),
            pltpu.VMEM((16, 32), jnp.int32),
            pltpu.VMEM((3, 8, 512), F32),
            pltpu.VMEM((8, 27, 64, 64), F32),
            pltpu.VMEM((8, 32, 32, 48), F32),
            pltpu.VMEM((32, 32, 48), F32),
            pltpu.VMEM((16, 32, 32), F32),
            pltpu.VMEM((8, 32, 64), F32),
            pltpu.VMEM((8, 32, 32), F32),
            pltpu.VMEM((1, 32, 32), F32),
            pltpu.VMEM((1, 32, 32), F32),
            pltpu.VMEM((8, 32, 32), F32),
            pltpu.VMEM((8, 32, 64), F32),
            pltpu.VMEM((2, 4, 4, ROWS, 256), F32),
            pltpu.VMEM((8, 2, 256), F32),
            pltpu.VMEM((2, 25, 8, 128), F32),
            pltpu.VMEM((8, 512), F32),
            pltpu.VMEM((768, 1024), BF16),
            pltpu.VMEM((128, 256), BF16),
            pltpu.VMEM((3, 448, 256), F32),
            pltpu.VMEM((2048, 256), BF16),
            pltpu.VMEM((2048, 256), BF16),
            pltpu.VMEM((2048, 128), BF16),
            pltpu.VMEM((2048, 128), BF16),
            pltpu.VMEM((384, 512), BF16),
            pltpu.VMEM((384, 512), BF16),
            pltpu.SemaphoreType.DMA((17,)),
            pltpu.SemaphoreType.DMA((4,)),
            pltpu.SemaphoreType.DMA((2,)),
            pltpu.SemaphoreType.DMA((2,)),
            pltpu.SemaphoreType.DMA((Z, 2)),
            pltpu.SemaphoreType.DMA((Z, 2)),
            pltpu.SemaphoreType.DMA((COPIES,)),
            pltpu.SemaphoreType.DMA((COPIES,)),
            pltpu.VMEM((2, 16, 128), F32),
            pltpu.SemaphoreType.DMA((2,)),
            pltpu.SemaphoreType.DMA((2,)),
            pltpu.SemaphoreType.REGULAR((RELATIONS,)),
        ],
        compiler_params=pltpu.CompilerParams(
            collective_id=0, has_side_effects=True, vmem_limit_bytes=60 * 2**20
        ),
    )(
        near_list,
        near_count,
        leaf_count,
        mid_count.reshape(1, 1),
        leaf_list,
        mid_list,
        top_list.T,
        x_block,
        near_tiles,
        leaf_tiles.transpose(0, 2, 3, 1),
        mid_tiles[0].transpose(1, 2, 0),
        top_tiles,
        leaf_in.transpose(0, 2, 1),
        leaf_up,
        mid_up,
        mid_down,
        leaf_down,
        leaf_out.transpose(0, 2, 1),
    )


def solution(mesh):
    placed = (
        P(None, "cluster"),
        P("cluster", None, None, None),
        P("cluster", None),
        P("cluster"),
        P("cluster", None, None),
        P("cluster", None, None),
        P("cluster", None, None),
        P("cluster", None, None, None),
        P("cluster", None),
        P("cluster"),
        P("cluster", None, None, None),
        P("cluster", None),
        P("cluster"),
        P(),
        P(),
        P("cluster", None, None),
        P("cluster", None, None),
        P("cluster", None, None),
    )
    return jax.shard_map(
        on_device, mesh=mesh, in_specs=placed, out_specs=P(None, "cluster"), check_vma=False
    )
```

```python
import functools

import jax
import jax.numpy as jnp
from jax import lax
from jax.experimental import pallas as pl
from jax.experimental.pallas import tpu as pltpu
from jax.sharding import PartitionSpec as P

F32 = jnp.float32
BF16 = jnp.bfloat16
MESH = pl.DeviceIdType.MESH

X, Y, Z = 4, 4, 8
ROWS = 80

EARLY = 4
PARTS = (pl.ds(0, 8 * EARLY), pl.ds(8 * EARLY, ROWS - 8 * EARLY), pl.ds(0, ROWS))
U_ID, V_ID = 0, 3
COPIES = 15
REL_U, REL_V, REL_SIB, REL_RIGHT, REL_LEFT = 8, 11, 14, 15, 16
RELATIONS = 17


def mod(a, n):
    return lax.rem(a + n, n)


def stacked(a):
    hi = a.astype(BF16).astype(F32)
    return jnp.concatenate([hi, a - hi], axis=0).astype(BF16)


def split(b):
    hi = b.astype(BF16)
    return hi, (b - hi.astype(F32)).astype(BF16)


def dot(a, b):
    return jnp.dot(a, b, preferred_element_type=F32)


def product2(a, hi, lo):
    both = stacked(a)
    out = dot(both, hi) + dot(both, lo)
    half = out.shape[0] // 2
    return out[:half] + out[half:]


def product(a, b):
    return product2(a, *split(b))


def iota(shape, dim):
    return lax.broadcasted_iota(jnp.int32, shape, dim)


def kernel(
    near_list_hbm,
    near_count_hbm,
    leaf_count_hbm,
    mid_count_hbm,
    leaf_list_hbm,
    mid_list_hbm,
    top_list_hbm,
    x_hbm,
    near_hbm,
    leaf_hbm,
    mid_hbm,
    top_hbm,
    lin_hbm,
    lup_hbm,
    mup_hbm,
    mdn_hbm,
    ldn_hbm,
    lout_hbm,
    out_ref,
    near_list,
    near_count,
    leaf_count,
    mid_count,
    leaf_list,
    mid_list,
    top_list,
    xbuf,
    near_v,
    leaf_v,
    mid_v,
    top_v,
    lin_v,
    lup_v,
    mup_v,
    mdn_v,
    ldn_v,
    lout_v,
    coef,
    stage,
    xe,
    near_acc,
    onehot,
    onehot2,
    picked,
    whi,
    wlo,
    w2hi,
    w2lo,
    ohi,
    olo,
    load_sem,
    near_sem,
    halo_send,
    halo_recv,
    z_send,
    z_recv,
    col_send,
    col_recv,
    wanted_rows,
    swap_send,
    swap_recv,
    ready_sem,
):
    me = lax.axis_index("cluster")
    c = lax.rem(me, 2)
    z = lax.rem(lax.div(me, 2), Z)
    y = lax.rem(lax.div(me, 2 * Z), Y)
    x = lax.div(me, 2 * Z * Y)
    flip = 1 - c
    v = x + flip * (y - x)
    u = y + flip * (x - y)

    def device(vv, uu, zz):
        xx = vv + flip * (uu - vv)
        yy = uu + flip * (vv - uu)
        return ((xx * Y + yy) * Z + zz) * 2 + c

    sibling = me + 1 - 2 * c
    right = mod(me + 1, 256)
    left = mod(me - 1, 256)

    def load(i, source, target):
        copy = pltpu.make_async_copy(source, target, load_sem.at[i])
        copy.start()
        return copy

    load_x = load(0, x_hbm, xbuf.at[1])
    load_lin = load(1, lin_hbm, lin_v)
    load_lup = load(2, lup_hbm, lup_v)
    load_mup = load(3, mup_hbm, mup_v)
    up, um, u2 = mod(u + 1, 4), mod(u - 1, 4), mod(u + 2, 4)
    vp, vm, v2 = mod(v + 1, 4), mod(v - 1, 4), mod(v + 2, 4)
    dev_up, dev_um, dev_u2 = device(v, up, z), device(v, um, z), device(v, u2, z)
    dev_vp, dev_vm, dev_v2 = device(vp, u, z), device(vm, u, z), device(v2, u, z)

    def rank(dev):
        xx = lax.div(dev, 2 * Z * Y)
        yy = lax.rem(lax.div(dev, 2 * Z), Y)
        zz = lax.rem(lax.div(dev, 2), Z)
        return ((zz * Y + yy) * X + xx) * 2 + lax.rem(dev, 2)

    mine = rank(me)
    relations = [
        (REL_U, dev_u2, REL_U),
        (REL_U + 1, dev_up, REL_U + 2),
        (REL_U + 2, dev_um, REL_U + 1),
        (REL_V, dev_v2, REL_V),
        (REL_V + 1, dev_vp, REL_V + 2),
        (REL_V + 2, dev_vm, REL_V + 1),
        (REL_SIB, sibling, REL_SIB),
        (REL_RIGHT, right, REL_LEFT),
        (REL_LEFT, left, REL_RIGHT),
    ]
    relations += [(k, device(v, u, mod(z + k, Z)), Z - k) for k in range(1, Z)]
    relations = [(i, dev, rank(dev), back) for i, dev, back in relations]
    barrier = pltpu.get_barrier_semaphore()
    greetings = jnp.int32(0)
    for _, dev, theirs, _ in relations:
        greetings += (theirs < mine).astype(jnp.int32)

        @pl.when(mine < theirs)
        def _():
            pl.semaphore_signal(barrier, inc=1, device_id=(dev,), device_id_type=MESH)

    def ready(relation):
        for i, _, theirs, _ in relations:
            if i == relation:

                @pl.when(mine < theirs)
                def _():
                    pl.semaphore_wait(ready_sem.at[i], 1)

    load_x.wait()
    load_lin.wait()
    load_lup.wait()
    load_mup.wait()
    zeros64 = jnp.zeros((32, 64), F32)
    r_parts = []
    for i in range(4):
        block = jnp.concatenate(
            [
                jnp.concatenate([lin_v[2 * i], zeros64], axis=1),
                jnp.concatenate([zeros64, lin_v[2 * i + 1]], axis=1),
            ],
            axis=0,
        )
        hi, lo = split(block)
        both = stacked(xbuf[1, :, i * 128 : (i + 1) * 128])
        nt = functools.partial(
            lax.dot_general,
            dimension_numbers=(((1,), (1,)), ((), ())),
            preferred_element_type=F32,
        )
        part = nt(both, hi) + nt(both, lo)
        r_parts.append(part[:8] + part[8:])
    r = jnp.concatenate(r_parts, axis=1)
    lup = lup_v[...].reshape(256, 32)
    both_up = jnp.concatenate([lup, product(lup, mup_v[0])], axis=1)
    spread = (iota((32, 256), 0) % 8 == iota((32, 256), 1) % 8).astype(BF16)
    same = iota((32, 256), 0) == iota((32, 256), 1) // 8

    def flat(a):
        n = a.shape[1] // 32
        if n % 4:
            a = jnp.concatenate([a, jnp.zeros((8, 32 * (4 - n % 4)), F32)], axis=1)
        hi = a.astype(BF16).astype(F32)
        rest = a - hi
        mid = rest.astype(BF16).astype(F32)
        parts = jnp.concatenate([hi, mid, rest - mid, jnp.zeros_like(a)], axis=0)
        rows = dot(jnp.transpose(parts).astype(BF16), spread)[: 32 * n]
        return jnp.sum(jnp.where(same[None], rows.reshape(n, 32, 256), 0.0), axis=1)

    my_rows = pl.ds(pl.multiple_of(z * 8, 8), 8)
    coef[c, v, u, my_rows, :] = flat(r)

    @pl.when(greetings > 0)
    def _():
        pl.semaphore_wait(barrier, greetings)

    for _, dev, theirs, back in relations:

        @pl.when(theirs < mine)
        def _():
            pl.semaphore_signal(
                ready_sem.at[back], inc=1, device_id=(dev,), device_id_type=MESH
            )

    def halo(i, source, target, dev):
        return pltpu.make_async_remote_copy(
            src_ref=xbuf.at[source],
            dst_ref=xbuf.at[target],
            send_sem=halo_send.at[i],
            recv_sem=halo_recv.at[i],
            device_id=(dev,),
            device_id_type=MESH,
        )

    def along_z(k, zz, dev):
        return (
            pltpu.make_async_remote_copy(
                src_ref=coef.at[c, v, u, pl.ds(pl.multiple_of(zz * 8, 8), 8)],
                dst_ref=coef.at[c, v, u, pl.ds(pl.multiple_of(zz * 8, 8), 8)],
                send_sem=z_send.at[k, 0],
                recv_sem=z_recv.at[k, 0],
                device_id=(dev,),
                device_id_type=MESH,
            ),
            pltpu.make_async_remote_copy(
                src_ref=stage.at[zz],
                dst_ref=stage.at[zz],
                send_sem=z_send.at[k, 1],
                recv_sem=z_recv.at[k, 1],
                device_id=(dev,),
                device_id_type=MESH,
            ),
        )

    halo_to = ((right, rank(right)), (left, rank(left)))
    for i, (dev, theirs) in enumerate(halo_to):

        @pl.when(theirs < mine)
        def _():
            halo(i, 1, 2 * i, dev).start()

    def to_plane(zz):
        k = mod(zz - z, Z)

        @pl.when(zz > z)
        def _():
            pl.semaphore_wait(ready_sem.at[k], 1)

        @pl.when(zz != z)
        def _():
            for copy in along_z(k, z, device(v, u, zz)):
                copy.start()

    def from_plane(zz, part):
        @pl.when(zz != z)
        def _():
            along_z(mod(z - zz, Z), zz, me)[part].wait_recv()

    stage[z] = flat(product(r, both_up))
    sends = []
    for zz in range(Z):
        to_plane(zz)
    load_lists = [
        load(10, leaf_count_hbm, leaf_count),
        load(11, mid_count_hbm, mid_count),
        load(12, leaf_list_hbm, leaf_list),
        load(13, mid_list_hbm, mid_list),
        load(14, top_list_hbm, top_list),
        load(15, near_list_hbm, near_list),
        load(16, near_count_hbm, near_count),
    ]
    load_near = []
    for i in range(4):
        copy = pltpu.make_async_copy(
            near_hbm.at[pl.ds(2 * i, 2)], near_v.at[pl.ds(2 * i, 2)], near_sem.at[i]
        )
        copy.start()
        load_near.append(copy)
    load_leaf = load(4, leaf_hbm, leaf_v)
    load_mid = load(5, mid_hbm, mid_v)
    load_top = load(6, top_hbm.at[lax.div(me, 8)], top_v)
    load_mdn = load(7, mdn_hbm, mdn_v)
    load_ldn = load(8, ldn_hbm, ldn_v)
    load_lout = load(9, lout_hbm, lout_v)

    def column(part, i, vv, uu, dev):
        ref = coef.at[c, vv, uu, PARTS[part]]
        sems = min(part, 1)
        return pltpu.make_async_remote_copy(
            src_ref=ref,
            dst_ref=ref,
            send_sem=col_send.at[sems, i],
            recv_sem=col_recv.at[sems, i],
            device_id=(dev,),
            device_id_type=MESH,
        )

    def along_u(part):
        for i, dev in ((1, dev_up), (2, dev_um), (0, dev_u2)):
            column(part, U_ID + i, v, u, dev).start()

    def along_v(part, k, uu):
        for i, dev in ((1, dev_vp), (2, dev_vm), (0, dev_v2)):
            column(part, V_ID + 3 * k + i, v, uu, dev).start()

    def turn(part):
        for k, i, uu in ((1, 1, um), (2, 2, up), (3, 0, u2)):
            column(part, U_ID + i, v, uu, me).wait_recv()
            along_v(part, k, uu)

    def from_v(part, k, uu):
        for i, vv in ((1, vm), (2, vp), (0, v2)):
            column(part, V_ID + 3 * k + i, vv, uu, me).wait_recv()

    def by_plane(step, first=None):
        @pl.when(z < EARLY)
        def _():
            if first is not None:
                first()
            step(1)

        @pl.when(z >= EARLY)
        def _():
            step(2)

    def place(s, shift):
        cc = (s >> shift) & 1
        zz = (s >> (shift + 1)) & 7
        yy = (s >> (shift + 4)) & 3
        xx = (s >> (shift + 6)) & 3
        vv = jnp.where(cc == 1, xx, yy)
        uu = jnp.where(cc == 1, yy, xx)
        return cc, uu * 32 + vv * 8 + zz

    def live_of(counts, width):
        n = len(counts)
        row = iota((n, width), 0)
        cap = jnp.zeros((n, width), jnp.int32)
        for i, count in enumerate(counts):
            cap = jnp.where(row == i, count, cap)
        return iota((n, width), 1) < cap

    def slots():
        s = leaf_list[...]
        cc, k = place(s, 3)
        k = cc * 1024 + k * 8 + (s & 7)
        k = jnp.where(live_of([leaf_count[i] for i in range(8)], 48), k, -1)
        cc, km = place(mid_list[...], 0)
        km = cc * 256 + (km >> 3) * 16 + (km & 7)
        km = jnp.where(iota((1, 48), 1) < mid_count[0, 0], km, -1)
        both = jnp.concatenate([k, jnp.broadcast_to(km, (8, 48))], axis=0)
        pad = jnp.full((16, 80), -1, jnp.int32)
        wanted_rows[0] = jnp.concatenate([both, pad], axis=1).astype(F32)

    def list_copy():
        return pltpu.make_async_remote_copy(
            src_ref=wanted_rows.at[0],
            dst_ref=wanted_rows.at[1],
            send_sem=swap_send.at[0],
            recv_sem=swap_recv.at[0],
            device_id=(sibling,),
            device_id_type=MESH,
        )

    def one_hot(side):
        cols = jnp.transpose(wanted_rows[side])
        start = (c * 1024).astype(F32)
        lanes = iota((48, 256), 1).astype(F32)
        for l in range(8):
            col = jnp.broadcast_to(cols[:48, l : l + 1], (48, 256)) - start
            rows = slice(side * 384 + l * 48, side * 384 + (l + 1) * 48)
            for t in range(4):
                onehot[rows, t * 256 : (t + 1) * 256] = jnp.where(
                    lanes + (t * 256.0) == col, 1.0, 0.0
                ).astype(BF16)
        start = (c * 256).astype(F32)
        col = jnp.broadcast_to(cols[:48, 8:9], (48, 256)) - start
        onehot2[side * 64 : side * 64 + 48, :] = jnp.where(
            lanes == col, 1.0, 0.0
        ).astype(BF16)
        wanted = jnp.where(iota((16, 32), 1) == lax.div(me, 8), top_list[...], 0)
        wanted = jnp.sum(wanted.astype(F32), axis=1, keepdims=True)
        k = iota((16, 256), 1)
        uu, vv = (k >> 6) & 3, (k >> 4) & 3
        xx = vv + flip * (uu - vv)
        yy = uu + flip * (vv - uu)
        top = (xx * 4 + yy) * 2 + ((k & 7) >> 2)
        top = jnp.where((k & 8) == 8, top, -1).astype(F32)
        onehot2[side * 64 + 48 : side * 64 + 64, :] = jnp.where(
            top == jnp.broadcast_to(wanted, (16, 256)), 1.0, 0.0
        ).astype(BF16)

    for copy in load_lists:
        copy.wait()
    slots()
    ready(REL_SIB)
    list_copy().start()
    one_hot(0)
    for i, (dev, theirs) in enumerate(halo_to):

        @pl.when(mine < theirs)
        def _():
            pl.semaphore_wait(ready_sem.at[REL_RIGHT + i], 1)
            halo(i, 1, 2 * i, dev).start()

    for i in range(3):
        ready(REL_U + i)
    for zz in range(EARLY):
        from_plane(zz, 0)

    @pl.when(z < EARLY)
    def _():
        along_u(0)

    for zz in range(EARLY, Z):
        from_plane(zz, 0)
    for zz in range(Z):
        from_plane(zz, 1)
    coef[c, v, u, 64:72, :] = stage[:, 0, :]
    coef[c, v, u, 72:80, :] = stage[:, 1, :]

    by_plane(along_u)
    list_copy().wait_recv()
    one_hot(1)

    for i, (source, target) in enumerate([(1, 0), (1, 2)]):
        halo(i, target, target, me).wait_recv()
    low = iota((8, 128), 1) < 64
    xe[0, 24] = jnp.zeros((8, 128), F32)
    xe[1, 24] = jnp.zeros((8, 128), F32)
    for i in range(12):
        tile = xbuf[i // 4, :, (i % 4) * 128 : (i % 4 + 1) * 128]
        turned = pltpu.roll(tile, 64, 1)
        xe[0, 2 * i] = tile
        xe[1, 2 * i] = turned
        xe[0, 2 * i + 1] = turned
        xe[1, 2 * i + 1] = tile
    base = me * 8 - 8

    def near_pair(i):
        outs = []
        for l in (2 * i, 2 * i + 1):
            count = near_count[l]

            def pick(n, side):
                s = jnp.clip(near_list[l, n] - base, 0, 23)
                return xe[side, jnp.where(n < count, s, 24)]

            parts = [
                jnp.where(low, pick(n, 0), pick(n + 1, 1)) for n in range(0, 26, 2)
            ]
            parts.append(pick(26, 0)[:, :64])
            lhs = jnp.concatenate(parts, axis=1)
            outs.append(product(lhs, near_v[l].reshape(27 * 64, 64)))
        near_acc[:, i * 128 : (i + 1) * 128] = jnp.concatenate(outs, axis=1)

    for i in range(4):
        load_near[i].wait()
        near_pair(i)

    for i in range(3):
        ready(REL_V + i)

    def early_v():
        along_v(0, 0, u)
        turn(0)

    by_plane(lambda part: along_v(part, 0, u), early_v)
    by_plane(turn)

    load_leaf.wait()
    load_mid.wait()
    load_top.wait()

    def pack(cp):
        gap = jnp.zeros((32, 16), F32)
        blocks = []
        for l in range(8):
            first, other = (2 * cp, 2 * cp + 1) if l % 2 == 0 else (2 * cp + 1, 2 * cp)
            blocks.append(
                jnp.concatenate([leaf_v[l, first], gap, leaf_v[l, other], gap], axis=1)
            )
        hi, lo = split(jnp.transpose(jnp.concatenate(blocks, axis=0)))
        rows = pl.ds(pl.multiple_of(cp * 128, 128), 128)
        whi[rows, :] = hi
        wlo[rows, :] = lo
        block = jnp.concatenate([mid_v[2 * cp], gap, mid_v[2 * cp + 1], gap], axis=1)
        block = jnp.transpose(
            jnp.concatenate([block, jnp.zeros((96, 128), F32)], axis=0)
        )
        rest = jnp.zeros((48, 32), F32)
        top = jnp.concatenate(
            [top_v[:, 2 * cp + 1, :], rest, top_v[:, 2 * cp, :], rest], axis=0
        )
        top = jnp.concatenate(
            [jnp.zeros((128, 32), F32), top, jnp.zeros((128, 64), F32)], axis=1
        )
        hi, lo = split(block + top)
        w2hi[rows, :] = hi
        w2lo[rows, :] = lo

    lax.fori_loop(0, 16, lambda i, _: (pack(i), 0)[1], 0)

    load_mdn.wait()
    load_ldn.wait()
    load_lout.wait()
    wide = []
    for l in range(8):
        pieces = [lout_v[l]]
        if l:
            pieces.insert(0, jnp.zeros((32, 64 * l), F32))
        if l < 7:
            pieces.append(jnp.zeros((32, 64 * (7 - l)), F32))
        wide.append(jnp.concatenate(pieces, axis=1))
    wide = jnp.concatenate(wide, axis=0)
    down = product(jnp.transpose(ldn_v[...].reshape(256, 32)), wide)
    down2 = product(jnp.transpose(mdn_v[0]), down)
    for rows, value in (
        (pl.ds(0, 256), wide),
        (pl.ds(256, 32), down),
        (pl.ds(288, 32), down2),
        (pl.ds(320, 64), jnp.zeros((64, 512), F32)),
    ):
        hi, lo = split(value)
        ohi[rows, :] = hi
        olo[rows, :] = lo

    def plane(uu, side, first):
        hi, lo = split(coef[c, :, uu, 0:64, :].reshape(256, 256))
        lanes = pl.ds(pl.multiple_of(uu * 256, 256), 256)
        rows = onehot[side * 384 : (side + 1) * 384, lanes]
        part = dot(rows, hi) + dot(rows, lo)
        if first:
            picked[side, 0:384, :] = part
        else:
            picked[side, 0:384, :] += part

    def upper(side):
        hi, lo = split(coef[c, :, :, 64:80, :].swapaxes(0, 1).reshape(256, 256))
        rows = onehot2[side * 64 : (side + 1) * 64, :]
        picked[side, 384:448, :] = dot(rows, hi) + dot(rows, lo)

    def swap():
        return pltpu.make_async_remote_copy(
            src_ref=picked.at[1],
            dst_ref=picked.at[2],
            send_sem=swap_send.at[1],
            recv_sem=swap_recv.at[1],
            device_id=(sibling,),
            device_id_type=MESH,
        )

    for k, uu in enumerate([u, um, up, u2]):
        by_plane(lambda part: from_v(part, k, uu), lambda: from_v(0, k, uu))
        if k < 3:
            plane(uu, 1, k == 0)
            plane(uu, 0, k == 0)
    upper(1)
    plane(u2, 1, False)
    swap().start()
    upper(0)
    plane(u2, 0, False)
    swap().wait_recv()
    total = picked[0] + picked[2]

    gap = jnp.zeros((16, 256), F32)
    turned = []
    for i in range(5):
        first, second = total[96 * i : 96 * i + 48], total[96 * i + 48 : 96 * i + 96]
        if i == 4:
            second = jnp.concatenate([second, gap, gap], axis=0)
        turned.append(jnp.transpose(jnp.concatenate([first, gap, second, gap], axis=0)))
    lhs = []
    for t in turned:
        even, odd = [], []
        for cp in range(16):
            a = t[16 * cp : 16 * cp + 8]
            b = pltpu.roll(t[16 * cp + 8 : 16 * cp + 16], 64, 1)
            even.append(jnp.where(low, a, b))
            odd.append(jnp.where(low, b, a))
        lhs += [jnp.concatenate(even, axis=1), jnp.concatenate(odd, axis=1)]
    far = product2(jnp.concatenate(lhs[:8], axis=0), whi[...], wlo[...])
    far = far.reshape(8, 8, 256)
    own = iota((8, 8, 256), 2) // 32 == iota((8, 8, 256), 0)
    far = jnp.sum(jnp.where(own, far, 0.0), axis=0)
    high = product2(jnp.concatenate(lhs[8:], axis=0), w2hi[...], w2lo[...])
    high = jnp.where(iota((8, 128), 1) < 32, high[:8], high[8:])
    field = jnp.concatenate([far, high], axis=1)
    out_ref[...] = near_acc[...] + product2(field, ohi[...], olo[...])

    for copy in sends + [list_copy(), swap()]:
        copy.wait_send()

    def sent(part):
        for i in range(COPIES):
            column(part, i, v, u, me).wait_send()

    by_plane(sent, lambda: sent(0))
    for i in range(2):
        halo(i, 1, 2 * i, me).wait_send()
    for k in range(1, Z):
        for copy in along_z(k, z, me):
            copy.wait_send()


def on_device(
    x_block,
    near_tiles,
    near_list,
    near_count,
    leaf_in,
    leaf_up,
    mid_up,
    leaf_tiles,
    leaf_list,
    leaf_count,
    mid_tiles,
    mid_list,
    mid_count,
    top_tiles,
    top_list,
    mid_down,
    leaf_down,
    leaf_out,
):
    vmem = pl.BlockSpec(memory_space=pltpu.VMEM)
    hbm = pl.BlockSpec(memory_space=pltpu.HBM)
    return pl.pallas_call(
        kernel,
        out_shape=pltpu.VMEM((8, 512), F32),
        in_specs=[hbm] * 18,
        out_specs=vmem,
        scratch_shapes=[
            pltpu.SMEM((8, 27), jnp.int32),
            pltpu.SMEM((8,), jnp.int32),
            pltpu.SMEM((8,), jnp.int32),
            pltpu.SMEM((1, 1), jnp.int32),
            pltpu.VMEM((8, 48), jnp.int32),
            pltpu.VMEM((1, 48), jnp.int32),
            pltpu.VMEM((16, 32), jnp.int32),
            pltpu.VMEM((3, 8, 512), F32),
            pltpu.VMEM((8, 27, 64, 64), F32),
            pltpu.VMEM((8, 32, 32, 48), F32),
            pltpu.VMEM((32, 32, 48), F32),
            pltpu.VMEM((16, 32, 32), F32),
            pltpu.VMEM((8, 32, 64), F32),
            pltpu.VMEM((8, 32, 32), F32),
            pltpu.VMEM((1, 32, 32), F32),
            pltpu.VMEM((1, 32, 32), F32),
            pltpu.VMEM((8, 32, 32), F32),
            pltpu.VMEM((8, 32, 64), F32),
            pltpu.VMEM((2, 4, 4, ROWS, 256), F32),
            pltpu.VMEM((8, 2, 256), F32),
            pltpu.VMEM((2, 25, 8, 128), F32),
            pltpu.VMEM((8, 512), F32),
            pltpu.VMEM((768, 1024), BF16),
            pltpu.VMEM((128, 256), BF16),
            pltpu.VMEM((3, 448, 256), F32),
            pltpu.VMEM((2048, 256), BF16),
            pltpu.VMEM((2048, 256), BF16),
            pltpu.VMEM((2048, 128), BF16),
            pltpu.VMEM((2048, 128), BF16),
            pltpu.VMEM((384, 512), BF16),
            pltpu.VMEM((384, 512), BF16),
            pltpu.SemaphoreType.DMA((17,)),
            pltpu.SemaphoreType.DMA((4,)),
            pltpu.SemaphoreType.DMA((2,)),
            pltpu.SemaphoreType.DMA((2,)),
            pltpu.SemaphoreType.DMA((Z, 2)),
            pltpu.SemaphoreType.DMA((Z, 2)),
            pltpu.SemaphoreType.DMA((2, COPIES)),
            pltpu.SemaphoreType.DMA((2, COPIES)),
            pltpu.VMEM((2, 16, 128), F32),
            pltpu.SemaphoreType.DMA((2,)),
            pltpu.SemaphoreType.DMA((2,)),
            pltpu.SemaphoreType.REGULAR((RELATIONS,)),
        ],
        compiler_params=pltpu.CompilerParams(
            collective_id=0, has_side_effects=True, vmem_limit_bytes=60 * 2**20
        ),
    )(
        near_list,
        near_count,
        leaf_count,
        mid_count.reshape(1, 1),
        leaf_list,
        mid_list,
        top_list.T,
        x_block,
        near_tiles,
        leaf_tiles.transpose(0, 2, 3, 1),
        mid_tiles[0].transpose(1, 2, 0),
        top_tiles,
        leaf_in.transpose(0, 2, 1),
        leaf_up,
        mid_up,
        mid_down,
        leaf_down,
        leaf_out.transpose(0, 2, 1),
    )


def solution(mesh):
    placed = (
        P(None, "cluster"),
        P("cluster", None, None, None),
        P("cluster", None),
        P("cluster"),
        P("cluster", None, None),
        P("cluster", None, None),
        P("cluster", None, None),
        P("cluster", None, None, None),
        P("cluster", None),
        P("cluster"),
        P("cluster", None, None, None),
        P("cluster", None),
        P("cluster"),
        P(),
        P(),
        P("cluster", None, None),
        P("cluster", None, None),
        P("cluster", None, None),
    )
    return jax.shard_map(
        on_device, mesh=mesh, in_specs=placed, out_specs=P(None, "cluster"), check_vma=False
    )
```

```python
import functools

import jax
import jax.numpy as jnp
from jax import lax
from jax.experimental import pallas as pl
from jax.experimental.pallas import tpu as pltpu
from jax.sharding import PartitionSpec as P

F32 = jnp.float32
BF16 = jnp.bfloat16
MESH = pl.DeviceIdType.MESH

X, Y, Z = 4, 4, 8
ROWS = 80

EARLY = 4
PARTS = (pl.ds(0, 8 * EARLY), pl.ds(8 * EARLY, ROWS - 8 * EARLY), pl.ds(0, ROWS))
U_ID, V_ID = 0, 3
COPIES = 15
REL_U, REL_V, REL_SIB, REL_RIGHT, REL_LEFT = 8, 11, 14, 15, 16
RELATIONS = 17


def mod(a, n):
    return lax.rem(a + n, n)


def stacked(a):
    hi = a.astype(BF16).astype(F32)
    return jnp.concatenate([hi, a - hi], axis=0).astype(BF16)


def split(b):
    hi = b.astype(BF16)
    return hi, (b - hi.astype(F32)).astype(BF16)


def dot(a, b):
    return jnp.dot(a, b, preferred_element_type=F32)


def product2(a, hi, lo):
    both = stacked(a)
    out = dot(both, hi) + dot(both, lo)
    half = out.shape[0] // 2
    return out[:half] + out[half:]


def product(a, b):
    return product2(a, *split(b))


def iota(shape, dim):
    return lax.broadcasted_iota(jnp.int32, shape, dim)


def kernel(
    near_list_hbm,
    near_count_hbm,
    leaf_count_hbm,
    mid_count_hbm,
    leaf_list_hbm,
    mid_list_hbm,
    top_list_hbm,
    x_hbm,
    near_hbm,
    leaf_hbm,
    mid_hbm,
    top_hbm,
    lin_hbm,
    lup_hbm,
    mup_hbm,
    mdn_hbm,
    ldn_hbm,
    lout_hbm,
    out_ref,
    near_list,
    near_count,
    leaf_count,
    mid_count,
    leaf_list,
    mid_list,
    top_list,
    xbuf,
    near_v,
    leaf_v,
    mid_v,
    top_v,
    lin_v,
    lup_v,
    mup_v,
    mdn_v,
    ldn_v,
    lout_v,
    coef,
    stage,
    xe,
    near_acc,
    onehot,
    onehot2,
    picked,
    whi,
    wlo,
    w2hi,
    w2lo,
    ohi,
    olo,
    load_sem,
    near_sem,
    halo_send,
    halo_recv,
    z_send,
    z_recv,
    col_send,
    col_recv,
    wanted_rows,
    swap_send,
    swap_recv,
    ready_sem,
):
    me = lax.axis_index("cluster")
    c = lax.rem(me, 2)
    z = lax.rem(lax.div(me, 2), Z)
    y = lax.rem(lax.div(me, 2 * Z), Y)
    x = lax.div(me, 2 * Z * Y)
    flip = 1 - c
    v = x + flip * (y - x)
    u = y + flip * (x - y)

    def device(vv, uu, zz):
        xx = vv + flip * (uu - vv)
        yy = uu + flip * (vv - uu)
        return ((xx * Y + yy) * Z + zz) * 2 + c

    sibling = me + 1 - 2 * c
    right = mod(me + 1, 256)
    left = mod(me - 1, 256)

    def load(i, source, target):
        copy = pltpu.make_async_copy(source, target, load_sem.at[i])
        copy.start()
        return copy

    load_x = load(0, x_hbm, xbuf.at[1])
    load_lin = load(1, lin_hbm, lin_v)
    load_lup = load(2, lup_hbm, lup_v)
    load_mup = load(3, mup_hbm, mup_v)
    up, um, u2 = mod(u + 1, 4), mod(u - 1, 4), mod(u + 2, 4)
    vp, vm, v2 = mod(v + 1, 4), mod(v - 1, 4), mod(v + 2, 4)
    dev_up, dev_um, dev_u2 = device(v, up, z), device(v, um, z), device(v, u2, z)
    dev_vp, dev_vm, dev_v2 = device(vp, u, z), device(vm, u, z), device(v2, u, z)

    def rank(dev):
        xx = lax.div(dev, 2 * Z * Y)
        yy = lax.rem(lax.div(dev, 2 * Z), Y)
        zz = lax.rem(lax.div(dev, 2), Z)
        return ((zz * Y + yy) * X + xx) * 2 + lax.rem(dev, 2)

    mine = rank(me)
    relations = [
        (REL_U, dev_u2, REL_U),
        (REL_U + 1, dev_up, REL_U + 2),
        (REL_U + 2, dev_um, REL_U + 1),
        (REL_V, dev_v2, REL_V),
        (REL_V + 1, dev_vp, REL_V + 2),
        (REL_V + 2, dev_vm, REL_V + 1),
        (REL_SIB, sibling, REL_SIB),
        (REL_RIGHT, right, REL_LEFT),
        (REL_LEFT, left, REL_RIGHT),
    ]
    relations += [(k, device(v, u, mod(z + k, Z)), Z - k) for k in range(1, Z)]
    relations = [(i, dev, rank(dev), back) for i, dev, back in relations]
    barrier = pltpu.get_barrier_semaphore()
    greetings = jnp.int32(0)
    for _, dev, theirs, _ in relations:
        greetings += (theirs < mine).astype(jnp.int32)

        @pl.when(mine < theirs)
        def _():
            pl.semaphore_signal(barrier, inc=1, device_id=(dev,), device_id_type=MESH)

    def ready(relation):
        for i, _, theirs, _ in relations:
            if i == relation:

                @pl.when(mine < theirs)
                def _():
                    pl.semaphore_wait(ready_sem.at[i], 1)

    load_x.wait()
    load_lin.wait()
    load_lup.wait()
    load_mup.wait()
    zeros64 = jnp.zeros((32, 64), F32)
    r_parts = []
    for i in range(4):
        block = jnp.concatenate(
            [
                jnp.concatenate([lin_v[2 * i], zeros64], axis=1),
                jnp.concatenate([zeros64, lin_v[2 * i + 1]], axis=1),
            ],
            axis=0,
        )
        hi, lo = split(block)
        both = stacked(xbuf[1, :, i * 128 : (i + 1) * 128])
        nt = functools.partial(
            lax.dot_general,
            dimension_numbers=(((1,), (1,)), ((), ())),
            preferred_element_type=F32,
        )
        part = nt(both, hi) + nt(both, lo)
        r_parts.append(part[:8] + part[8:])
    r = jnp.concatenate(r_parts, axis=1)
    lup = lup_v[...].reshape(256, 32)
    both_up = jnp.concatenate([lup, product(lup, mup_v[0])], axis=1)
    spread = (iota((32, 256), 0) % 8 == iota((32, 256), 1) % 8).astype(BF16)
    same = iota((32, 256), 0) == iota((32, 256), 1) // 8

    def flat(a):
        n = a.shape[1] // 32
        if n % 4:
            a = jnp.concatenate([a, jnp.zeros((8, 32 * (4 - n % 4)), F32)], axis=1)
        hi = a.astype(BF16).astype(F32)
        rest = a - hi
        mid = rest.astype(BF16).astype(F32)
        parts = jnp.concatenate([hi, mid, rest - mid, jnp.zeros_like(a)], axis=0)
        rows = dot(jnp.transpose(parts).astype(BF16), spread)[: 32 * n]
        return jnp.sum(jnp.where(same[None], rows.reshape(n, 32, 256), 0.0), axis=1)

    my_rows = pl.ds(pl.multiple_of(z * 8, 8), 8)
    coef[c, v, u, my_rows, :] = flat(r)

    @pl.when(greetings > 0)
    def _():
        pl.semaphore_wait(barrier, greetings)

    for _, dev, theirs, back in relations:

        @pl.when(theirs < mine)
        def _():
            pl.semaphore_signal(
                ready_sem.at[back], inc=1, device_id=(dev,), device_id_type=MESH
            )

    def halo(i, source, target, dev):
        return pltpu.make_async_remote_copy(
            src_ref=xbuf.at[source],
            dst_ref=xbuf.at[target],
            send_sem=halo_send.at[i],
            recv_sem=halo_recv.at[i],
            device_id=(dev,),
            device_id_type=MESH,
        )

    def along_z(k, zz, dev):
        return (
            pltpu.make_async_remote_copy(
                src_ref=coef.at[c, v, u, pl.ds(pl.multiple_of(zz * 8, 8), 8)],
                dst_ref=coef.at[c, v, u, pl.ds(pl.multiple_of(zz * 8, 8), 8)],
                send_sem=z_send.at[k, 0],
                recv_sem=z_recv.at[k, 0],
                device_id=(dev,),
                device_id_type=MESH,
            ),
            pltpu.make_async_remote_copy(
                src_ref=stage.at[zz],
                dst_ref=stage.at[zz],
                send_sem=z_send.at[k, 1],
                recv_sem=z_recv.at[k, 1],
                device_id=(dev,),
                device_id_type=MESH,
            ),
        )

    halo_to = ((right, rank(right)), (left, rank(left)))
    for i, (dev, theirs) in enumerate(halo_to):

        @pl.when(theirs < mine)
        def _():
            halo(i, 1, 2 * i, dev).start()

    def to_plane(zz):
        k = mod(zz - z, Z)

        @pl.when(zz > z)
        def _():
            pl.semaphore_wait(ready_sem.at[k], 1)

        @pl.when(zz != z)
        def _():
            for copy in along_z(k, z, device(v, u, zz)):
                copy.start()

    def from_plane(zz, part):
        @pl.when(zz != z)
        def _():
            along_z(mod(z - zz, Z), zz, me)[part].wait_recv()

    stage[z] = flat(product(r, both_up))
    sends = []
    for zz in range(Z):
        to_plane(zz)
    load_lists = [
        load(10, leaf_count_hbm, leaf_count),
        load(11, mid_count_hbm, mid_count),
        load(12, leaf_list_hbm, leaf_list),
        load(13, mid_list_hbm, mid_list),
        load(14, top_list_hbm, top_list),
        load(15, near_list_hbm, near_list),
        load(16, near_count_hbm, near_count),
    ]
    load_near = []
    for i in range(4):
        copy = pltpu.make_async_copy(
            near_hbm.at[pl.ds(2 * i, 2)], near_v.at[pl.ds(2 * i, 2)], near_sem.at[i]
        )
        copy.start()
        load_near.append(copy)
    load_leaf = load(4, leaf_hbm, leaf_v)
    load_mid = load(5, mid_hbm, mid_v)
    load_top = load(6, top_hbm.at[lax.div(me, 8)], top_v)
    load_mdn = load(7, mdn_hbm, mdn_v)
    load_ldn = load(8, ldn_hbm, ldn_v)
    load_lout = load(9, lout_hbm, lout_v)

    def column(part, i, vv, uu, dev):
        ref = coef.at[c, vv, uu, PARTS[part]]
        sems = min(part, 1)
        return pltpu.make_async_remote_copy(
            src_ref=ref,
            dst_ref=ref,
            send_sem=col_send.at[sems, i],
            recv_sem=col_recv.at[sems, i],
            device_id=(dev,),
            device_id_type=MESH,
        )

    def along_u(part):
        for i, dev in ((1, dev_up), (2, dev_um), (0, dev_u2)):
            column(part, U_ID + i, v, u, dev).start()

    def along_v(part, k, uu):
        for i, dev in ((1, dev_vp), (2, dev_vm), (0, dev_v2)):
            column(part, V_ID + 3 * k + i, v, uu, dev).start()

    def turn(part):
        for k, i, uu in ((1, 1, um), (2, 2, up), (3, 0, u2)):
            column(part, U_ID + i, v, uu, me).wait_recv()
            along_v(part, k, uu)

    def from_v(part, k, uu):
        for i, vv in ((1, vm), (2, vp), (0, v2)):
            column(part, V_ID + 3 * k + i, vv, uu, me).wait_recv()

    def by_plane(step, first=None):
        @pl.when(z < EARLY)
        def _():
            if first is not None:
                first()
            step(1)

        @pl.when(z >= EARLY)
        def _():
            step(2)

    def place(s, shift):
        cc = (s >> shift) & 1
        zz = (s >> (shift + 1)) & 7
        yy = (s >> (shift + 4)) & 3
        xx = (s >> (shift + 6)) & 3
        vv = jnp.where(cc == 1, xx, yy)
        uu = jnp.where(cc == 1, yy, xx)
        return cc, uu * 32 + vv * 8 + zz

    def live_of(counts, width):
        n = len(counts)
        row = iota((n, width), 0)
        cap = jnp.zeros((n, width), jnp.int32)
        for i, count in enumerate(counts):
            cap = jnp.where(row == i, count, cap)
        return iota((n, width), 1) < cap

    def slots():
        s = leaf_list[...]
        cc, k = place(s, 3)
        k = cc * 1024 + k * 8 + (s & 7)
        k = jnp.where(live_of([leaf_count[i] for i in range(8)], 48), k, -1)
        cc, km = place(mid_list[...], 0)
        km = cc * 256 + (km >> 3) * 16 + (km & 7)
        km = jnp.where(iota((1, 48), 1) < mid_count[0, 0], km, -1)
        both = jnp.concatenate([k, jnp.broadcast_to(km, (8, 48))], axis=0)
        pad = jnp.full((16, 80), -1, jnp.int32)
        wanted_rows[0] = jnp.concatenate([both, pad], axis=1).astype(F32)

    def list_copy():
        return pltpu.make_async_remote_copy(
            src_ref=wanted_rows.at[0],
            dst_ref=wanted_rows.at[1],
            send_sem=swap_send.at[0],
            recv_sem=swap_recv.at[0],
            device_id=(sibling,),
            device_id_type=MESH,
        )

    def one_hot(side):
        cols = jnp.transpose(wanted_rows[side])
        start = (c * 1024).astype(F32)
        lanes = iota((48, 256), 1).astype(F32)
        for l in range(8):
            col = jnp.broadcast_to(cols[:48, l : l + 1], (48, 256)) - start
            rows = slice(side * 384 + l * 48, side * 384 + (l + 1) * 48)
            for t in range(4):
                onehot[rows, t * 256 : (t + 1) * 256] = jnp.where(
                    lanes + (t * 256.0) == col, 1.0, 0.0
                ).astype(BF16)
        start = (c * 256).astype(F32)
        col = jnp.broadcast_to(cols[:48, 8:9], (48, 256)) - start
        onehot2[side * 64 : side * 64 + 48, :] = jnp.where(
            lanes == col, 1.0, 0.0
        ).astype(BF16)
        wanted = jnp.where(iota((16, 32), 1) == lax.div(me, 8), top_list[...], 0)
        wanted = jnp.sum(wanted.astype(F32), axis=1, keepdims=True)
        k = iota((16, 256), 1)
        uu, vv = (k >> 6) & 3, (k >> 4) & 3
        xx = vv + flip * (uu - vv)
        yy = uu + flip * (vv - uu)
        top = (xx * 4 + yy) * 2 + ((k & 7) >> 2)
        top = jnp.where((k & 8) == 8, top, -1).astype(F32)
        onehot2[side * 64 + 48 : side * 64 + 64, :] = jnp.where(
            top == jnp.broadcast_to(wanted, (16, 256)), 1.0, 0.0
        ).astype(BF16)

    for copy in load_lists:
        copy.wait()
    slots()
    ready(REL_SIB)
    list_copy().start()
    one_hot(0)
    for i, (dev, theirs) in enumerate(halo_to):

        @pl.when(mine < theirs)
        def _():
            pl.semaphore_wait(ready_sem.at[REL_RIGHT + i], 1)
            halo(i, 1, 2 * i, dev).start()

    for i in range(3):
        ready(REL_U + i)
    for zz in range(EARLY):
        from_plane(zz, 0)

    @pl.when(z < EARLY)
    def _():
        along_u(0)

    for zz in range(EARLY, Z):
        from_plane(zz, 0)
    for zz in range(Z):
        from_plane(zz, 1)
    coef[c, v, u, 64:72, :] = stage[:, 0, :]
    coef[c, v, u, 72:80, :] = stage[:, 1, :]

    by_plane(along_u)
    list_copy().wait_recv()
    one_hot(1)

    for i, (source, target) in enumerate([(1, 0), (1, 2)]):
        halo(i, target, target, me).wait_recv()
    low = iota((8, 128), 1) < 64
    xe[0, 24] = jnp.zeros((8, 128), F32)
    xe[1, 24] = jnp.zeros((8, 128), F32)
    for i in range(12):
        tile = xbuf[i // 4, :, (i % 4) * 128 : (i % 4 + 1) * 128]
        turned = pltpu.roll(tile, 64, 1)
        xe[0, 2 * i] = tile
        xe[1, 2 * i] = turned
        xe[0, 2 * i + 1] = turned
        xe[1, 2 * i + 1] = tile
    base = me * 8 - 8

    def near_pair(i):
        outs = []
        for l in (2 * i, 2 * i + 1):
            count = near_count[l]

            def pick(n, side):
                s = jnp.clip(near_list[l, n] - base, 0, 23)
                return xe[side, jnp.where(n < count, s, 24)]

            parts = [
                jnp.where(low, pick(n, 0), pick(n + 1, 1)) for n in range(0, 26, 2)
            ]
            parts.append(pick(26, 0)[:, :64])
            lhs = jnp.concatenate(parts, axis=1)
            outs.append(product(lhs, near_v[l].reshape(27 * 64, 64)))
        near_acc[:, i * 128 : (i + 1) * 128] = jnp.concatenate(outs, axis=1)

    for i in range(4):
        load_near[i].wait()
        near_pair(i)

    for i in range(3):
        ready(REL_V + i)

    def early_v():
        along_v(0, 0, u)
        turn(0)

    by_plane(lambda part: along_v(part, 0, u), early_v)
    by_plane(turn)

    load_leaf.wait()
    load_mid.wait()
    load_top.wait()

    def pack(cp):
        gap = jnp.zeros((32, 16), F32)
        blocks = []
        for l in range(8):
            first, other = (2 * cp, 2 * cp + 1) if l % 2 == 0 else (2 * cp + 1, 2 * cp)
            blocks.append(
                jnp.concatenate([leaf_v[l, first], gap, leaf_v[l, other], gap], axis=1)
            )
        hi, lo = split(jnp.transpose(jnp.concatenate(blocks, axis=0)))
        rows = pl.ds(pl.multiple_of(cp * 128, 128), 128)
        whi[rows, :] = hi
        wlo[rows, :] = lo
        block = jnp.concatenate([mid_v[2 * cp], gap, mid_v[2 * cp + 1], gap], axis=1)
        block = jnp.transpose(
            jnp.concatenate([block, jnp.zeros((96, 128), F32)], axis=0)
        )
        rest = jnp.zeros((48, 32), F32)
        top = jnp.concatenate(
            [top_v[:, 2 * cp + 1, :], rest, top_v[:, 2 * cp, :], rest], axis=0
        )
        top = jnp.concatenate(
            [jnp.zeros((128, 32), F32), top, jnp.zeros((128, 64), F32)], axis=1
        )
        hi, lo = split(block + top)
        w2hi[rows, :] = hi
        w2lo[rows, :] = lo

    lax.fori_loop(0, 16, lambda i, _: (pack(i), 0)[1], 0)

    load_mdn.wait()
    load_ldn.wait()
    load_lout.wait()
    wide = []
    for l in range(8):
        pieces = [lout_v[l]]
        if l:
            pieces.insert(0, jnp.zeros((32, 64 * l), F32))
        if l < 7:
            pieces.append(jnp.zeros((32, 64 * (7 - l)), F32))
        wide.append(jnp.concatenate(pieces, axis=1))
    wide = jnp.concatenate(wide, axis=0)
    down = product(jnp.transpose(ldn_v[...].reshape(256, 32)), wide)
    down2 = product(jnp.transpose(mdn_v[0]), down)
    for rows, value in (
        (pl.ds(0, 256), wide),
        (pl.ds(256, 32), down),
        (pl.ds(288, 32), down2),
        (pl.ds(320, 64), jnp.zeros((64, 512), F32)),
    ):
        hi, lo = split(value)
        ohi[rows, :] = hi
        olo[rows, :] = lo

    def plane(uu, side, first):
        hi, lo = split(coef[c, :, uu, 0:64, :].reshape(256, 256))
        lanes = pl.ds(pl.multiple_of(uu * 256, 256), 256)
        rows = onehot[side * 384 : (side + 1) * 384, lanes]
        part = dot(rows, hi) + dot(rows, lo)
        if first:
            picked[side, 0:384, :] = part
        else:
            picked[side, 0:384, :] += part

    def upper(side):
        hi, lo = split(coef[c, :, :, 64:80, :].swapaxes(0, 1).reshape(256, 256))
        rows = onehot2[side * 64 : (side + 1) * 64, :]
        picked[side, 384:448, :] = dot(rows, hi) + dot(rows, lo)

    def swap(part):
        rows = pl.ds(192 * part, 192 + 64 * part)
        return pltpu.make_async_remote_copy(
            src_ref=picked.at[1, rows],
            dst_ref=picked.at[2, rows],
            send_sem=swap_send.at[1 + part],
            recv_sem=swap_recv.at[1 + part],
            device_id=(sibling,),
            device_id_type=MESH,
        )

    for k, uu in enumerate([u, um, up, u2]):
        by_plane(lambda part: from_v(part, k, uu), lambda: from_v(0, k, uu))
        if k < 3:
            plane(uu, 1, k == 0)
            plane(uu, 0, k == 0)
    plane(u2, 1, False)
    swap(0).start()
    upper(1)
    swap(1).start()
    upper(0)
    plane(u2, 0, False)
    swap(0).wait_recv()
    swap(1).wait_recv()
    total = picked[0] + picked[2]

    gap = jnp.zeros((16, 256), F32)
    turned = []
    for i in range(5):
        first, second = total[96 * i : 96 * i + 48], total[96 * i + 48 : 96 * i + 96]
        if i == 4:
            second = jnp.concatenate([second, gap, gap], axis=0)
        turned.append(jnp.transpose(jnp.concatenate([first, gap, second, gap], axis=0)))
    lhs = []
    for t in turned:
        even, odd = [], []
        for cp in range(16):
            a = t[16 * cp : 16 * cp + 8]
            b = pltpu.roll(t[16 * cp + 8 : 16 * cp + 16], 64, 1)
            even.append(jnp.where(low, a, b))
            odd.append(jnp.where(low, b, a))
        lhs += [jnp.concatenate(even, axis=1), jnp.concatenate(odd, axis=1)]
    far = product2(jnp.concatenate(lhs[:8], axis=0), whi[...], wlo[...])
    far = far.reshape(8, 8, 256)
    own = iota((8, 8, 256), 2) // 32 == iota((8, 8, 256), 0)
    far = jnp.sum(jnp.where(own, far, 0.0), axis=0)
    high = product2(jnp.concatenate(lhs[8:], axis=0), w2hi[...], w2lo[...])
    high = jnp.where(iota((8, 128), 1) < 32, high[:8], high[8:])
    field = jnp.concatenate([far, high], axis=1)
    out_ref[...] = near_acc[...] + product2(field, ohi[...], olo[...])

    for copy in sends + [list_copy(), swap(0), swap(1)]:
        copy.wait_send()

    def sent(part):
        for i in range(COPIES):
            column(part, i, v, u, me).wait_send()

    by_plane(sent, lambda: sent(0))
    for i in range(2):
        halo(i, 1, 2 * i, me).wait_send()
    for k in range(1, Z):
        for copy in along_z(k, z, me):
            copy.wait_send()


def on_device(
    x_block,
    near_tiles,
    near_list,
    near_count,
    leaf_in,
    leaf_up,
    mid_up,
    leaf_tiles,
    leaf_list,
    leaf_count,
    mid_tiles,
    mid_list,
    mid_count,
    top_tiles,
    top_list,
    mid_down,
    leaf_down,
    leaf_out,
):
    vmem = pl.BlockSpec(memory_space=pltpu.VMEM)
    hbm = pl.BlockSpec(memory_space=pltpu.HBM)
    return pl.pallas_call(
        kernel,
        out_shape=pltpu.VMEM((8, 512), F32),
        in_specs=[hbm] * 18,
        out_specs=vmem,
        scratch_shapes=[
            pltpu.SMEM((8, 27), jnp.int32),
            pltpu.SMEM((8,), jnp.int32),
            pltpu.SMEM((8,), jnp.int32),
            pltpu.SMEM((1, 1), jnp.int32),
            pltpu.VMEM((8, 48), jnp.int32),
            pltpu.VMEM((1, 48), jnp.int32),
            pltpu.VMEM((16, 32), jnp.int32),
            pltpu.VMEM((3, 8, 512), F32),
            pltpu.VMEM((8, 27, 64, 64), F32),
            pltpu.VMEM((8, 32, 32, 48), F32),
            pltpu.VMEM((32, 32, 48), F32),
            pltpu.VMEM((16, 32, 32), F32),
            pltpu.VMEM((8, 32, 64), F32),
            pltpu.VMEM((8, 32, 32), F32),
            pltpu.VMEM((1, 32, 32), F32),
            pltpu.VMEM((1, 32, 32), F32),
            pltpu.VMEM((8, 32, 32), F32),
            pltpu.VMEM((8, 32, 64), F32),
            pltpu.VMEM((2, 4, 4, ROWS, 256), F32),
            pltpu.VMEM((8, 2, 256), F32),
            pltpu.VMEM((2, 25, 8, 128), F32),
            pltpu.VMEM((8, 512), F32),
            pltpu.VMEM((768, 1024), BF16),
            pltpu.VMEM((128, 256), BF16),
            pltpu.VMEM((3, 448, 256), F32),
            pltpu.VMEM((2048, 256), BF16),
            pltpu.VMEM((2048, 256), BF16),
            pltpu.VMEM((2048, 128), BF16),
            pltpu.VMEM((2048, 128), BF16),
            pltpu.VMEM((384, 512), BF16),
            pltpu.VMEM((384, 512), BF16),
            pltpu.SemaphoreType.DMA((17,)),
            pltpu.SemaphoreType.DMA((4,)),
            pltpu.SemaphoreType.DMA((2,)),
            pltpu.SemaphoreType.DMA((2,)),
            pltpu.SemaphoreType.DMA((Z, 2)),
            pltpu.SemaphoreType.DMA((Z, 2)),
            pltpu.SemaphoreType.DMA((2, COPIES)),
            pltpu.SemaphoreType.DMA((2, COPIES)),
            pltpu.VMEM((2, 16, 128), F32),
            pltpu.SemaphoreType.DMA((3,)),
            pltpu.SemaphoreType.DMA((3,)),
            pltpu.SemaphoreType.REGULAR((RELATIONS,)),
        ],
        compiler_params=pltpu.CompilerParams(
            collective_id=0, has_side_effects=True, vmem_limit_bytes=60 * 2**20
        ),
    )(
        near_list,
        near_count,
        leaf_count,
        mid_count.reshape(1, 1),
        leaf_list,
        mid_list,
        top_list.T,
        x_block,
        near_tiles,
        leaf_tiles.transpose(0, 2, 3, 1),
        mid_tiles[0].transpose(1, 2, 0),
        top_tiles,
        leaf_in.transpose(0, 2, 1),
        leaf_up,
        mid_up,
        mid_down,
        leaf_down,
        leaf_out.transpose(0, 2, 1),
    )


def solution(mesh):
    placed = (
        P(None, "cluster"),
        P("cluster", None, None, None),
        P("cluster", None),
        P("cluster"),
        P("cluster", None, None),
        P("cluster", None, None),
        P("cluster", None, None),
        P("cluster", None, None, None),
        P("cluster", None),
        P("cluster"),
        P("cluster", None, None, None),
        P("cluster", None),
        P("cluster"),
        P(),
        P(),
        P("cluster", None, None),
        P("cluster", None, None),
        P("cluster", None, None),
    )
    return jax.shard_map(
        on_device, mesh=mesh, in_specs=placed, out_specs=P(None, "cluster"), check_vma=False
    )
```
